512 devices in a mesh: gx: 32 (over y, z_hi, core), gy: 16 (over x, z_lo).
Axes of the slice: x: 4, y: 4, z: 16 (z_hi: 4, z_lo: 4; z = z_hi * 4 + z_lo), core: 2. Of those that a mesh axis runs over, the one named last changes fastest.
Arguments:
- pressure: float32 [512, 98304], P('gx', 'gy'), may hold values from -6 to 6
- previous: float32 [512, 98304], P('gx', 'gy'), may hold values from -6 to 6
- velocity: bfloat16 [512, 98304], P('gx', 'gy'), may hold values from 0.039794922 to 0.19921875
- tucker_core: bfloat16 [3, 384, 12288], P(None, 'gx', 'gy'), may hold values from -6 to 6
- first_factor: bfloat16 [512, 384], P('gx'), may hold values from -0.3125 to 0.3125
- second_factor: bfloat16 [1536, 384], P('gy'), may hold values from -0.3125 to 0.3125
- depth_factor: bfloat16 [64, 32], replicated, may hold values from -1 to 1
Outputs:
- image: float32 [512, 98304], P('gx', 'gy')
The draws below stay inside these ranges and needn't reach their ends.
All inputs are finite; a program needn't handle non-finite values.
Results may differ from the reference program's by a relative error of at most 0.00035.
Values may be sent and summed in bfloat16 or wider, within the bound.
A program may use at most 192 MiB of HBM per device.

```python
import math
import jax
import jax.numpy as jnp
from jax import lax

CX = 16
NZ = 64
R1 = 384
R2 = 384
R3 = 32
STEPS = 3
NX = 512
NY = 1536
N_GX = 32


def levels(stream_key, shape, pieces, low, largest):
    gain, own = 1.0, jax.random.fold_in(stream_key, 6)
    for dim, parts in pieces:
        steps = jnp.exp(jax.random.uniform(jax.random.fold_in(own, dim), (parts,), jnp.float32, low / len(pieces), largest / len(pieces)))
        gain = gain * jnp.repeat(steps, shape[dim] // parts).reshape([-1 if axis == dim else 1 for axis in range(len(shape))])
    return gain


def centred(own_key, extent, spread, limit, shards=(), held_as=jnp.bfloat16):
    drawn = jax.random.normal(own_key, extent, jnp.float32) * spread
    if len(shards) > 0:
        drawn = levels(own_key, extent, shards, -0.22, 0.18) * drawn
    return jnp.clip(drawn, min=-limit, max=limit).astype(held_as)


def setup_inputs(seed: int = 0) -> dict:
    keys = jax.random.split(jax.random.key(seed), 8)
    return {
        "pressure": centred(keys[0], (NX, NY * NZ), 1.0, 6.0, ((0, 32), (1, 16)), jnp.float32),
        "previous": centred(keys[1], (NX, NY * NZ), 1.0, 6.0, ((0, 32), (1, 16)), jnp.float32),
        "velocity": jnp.clip(jnp.exp(math.log(0.19921875) - 1.61066415 * jax.random.uniform(keys[2], (NX, NY * NZ), jnp.float32) ** levels(keys[2], (NX, NY * NZ), ((0, 32), (1, 16)), -0.2, 0.2)), 0.039794922, 0.19921875).astype(jnp.bfloat16),
        "tucker_core": centred(keys[3], (STEPS, R1, R2 * R3), 1.0, 6.0, ((1, 32), (2, 16))),
        "first_factor": centred(keys[4], (NX, R1), R1 ** -0.5, 0.3125, ((0, 32),)),
        "second_factor": centred(keys[5], (NY, R2), R2 ** -0.5, 0.3125, ((0, 16),)),
        "depth_factor": centred(keys[6], (NZ, R3), R3 ** -0.5, 1.0),
    }


STENCIL = (-205.0 / 72.0, 8.0 / 5.0, -1.0 / 5.0, 8.0 / 315.0, -1.0 / 560.0)
HIGH = lax.Precision.HIGHEST


def laplace(field):
    padded = jnp.pad(field, 4)
    size_x, size_y, size_z = field.shape
    total = 3.0 * STENCIL[0] * field
    for reach in range(1, 5):
        near = padded[4 + reach:4 + reach + size_x, 4:4 + size_y, 4:4 + size_z] + padded[4 - reach:4 - reach + size_x, 4:4 + size_y, 4:4 + size_z]
        near = near + padded[4:4 + size_x, 4 + reach:4 + reach + size_y, 4:4 + size_z] + padded[4:4 + size_x, 4 - reach:4 - reach + size_y, 4:4 + size_z]
        near = near + padded[4:4 + size_x, 4:4 + size_y, 4 + reach:4 + reach + size_z] + padded[4:4 + size_x, 4:4 + size_y, 4 - reach:4 - reach + size_z]
        total = total + STENCIL[reach] * near
    return total


def source_field(core_step, first_factor, second_factor, depth_factor):
    core_block = core_step.astype(jnp.float32).reshape(R1, R2, R3)
    second = second_factor.astype(jnp.float32)
    depth = depth_factor.astype(jnp.float32)

    def one_block(rows):
        partial_value = jnp.einsum("xa,abc->xbc", rows.astype(jnp.float32), core_block, precision=HIGH)
        mixed = jnp.einsum("xbc,yb->xyc", partial_value, second, precision=HIGH)
        return jnp.einsum("xyc,zc->xyz", mixed, depth, precision=HIGH)

    blocks = lax.map(one_block, first_factor.reshape(N_GX, CX, R1))
    return blocks.reshape(NX, NY, NZ)


def reference(pressure, previous, velocity, tucker_core, first_factor, second_factor, depth_factor):
    current = pressure.reshape(NX, NY, NZ)
    before = previous.reshape(NX, NY, NZ)
    speed = velocity.astype(jnp.float32).reshape(NX, NY, NZ)
    image = jnp.zeros((NX, NY, NZ), jnp.float32)
    for section in range(STEPS):
        following = 2.0 * current - before + speed * laplace(current)
        image = image + source_field(tucker_core[section], first_factor, second_factor, depth_factor) * following
        before = current
        current = following
    return image.reshape(NX, NY * NZ)
```

```python
import functools

import jax
import jax.numpy as jnp
import numpy as np
from jax import lax
from jax.experimental import pallas as pl
from jax.experimental.pallas import tpu as pltpu
from jax.sharding import PartitionSpec as P

STENCIL = (-205.0 / 72.0, 8.0 / 5.0, -1.0 / 5.0, 8.0 / 315.0, -1.0 / 560.0)
MESH = pl.DeviceIdType.MESH
F32, BF16 = jnp.float32, jnp.bfloat16

STEPS = 3
CX = 16
NZ = 64
YL = 96
TILES = YL * NZ // 128
POWER = 13.0
LIFT = 512.0


def constants():
    first = np.zeros((384, 768), np.float32)
    for core in range(2):
        for y in range(4):
            for zh in range(4):
                block = (y * 4 + zh) * 2 + core
                slot = (core * 4 + y) * 4 + zh
                for r in range(8):
                    first[block * 12 + r, slot * 8 + r] = 1.0
                for r in range(4):
                    first[block * 12 + 8 + r, 256 + slot * 8 + r] = 1.0
                    first[block * 12 + 8 + r, 512 + slot * 8 + 4 + r] = 1.0
    second = np.zeros((384, 384), np.float32)
    for block in range(16):
        for m in range(4):
            for q in range(6):
                second[block * 24 + 4 * q + m, block * 24 + 6 * m + q] = 1.0
    down = np.tile(np.eye(32, dtype=np.float32), (4, 1))
    across = np.tile(np.eye(64, dtype=np.float32), (1, 4))
    return tuple(jnp.asarray(a, BF16) for a in (first, second, down, across))


def dot(a, b):
    return lax.dot_general(a, b, (((1,), (0,)), ((), ())), preferred_element_type=F32)


def halves(a):
    high = a.astype(BF16)
    return high, (a - high.astype(F32)).astype(BF16)


def encode(value, scale):
    u = value * scale
    u2 = u * u
    u4 = u2 * u2
    return u4 * u4 * u4 * u


def decode(code, scale):
    size = jnp.abs(code)
    root = jnp.exp2(jnp.log2(jnp.maximum(size, 1e-38)) * (1.0 / POWER)) * scale
    root = jnp.where(size < 1e-37, 0.0, root)
    return jnp.where(code < 0.0, -root, root)


def kernel(
    pres, prev, vel, core, f1, f2, dep, pf1, pf2, down, across,
    out,
    pres_v, prev_v, vel_v, core_v, f1_v, f2_v, dep_v, pf1_v, pf2_v, down_v, across_v,
    kb, gb, fld, rolled, last, hxs, hxr, hys, hyr, v_s, w_s, g_s, t_s, bd_s, f1a_s, f1b_s, f2p_s,
    lsem, zs, zr, ys, yr, cs, cr, gzs, gzr, gxs, gxr, hxss, hxrs, hyss, hyrs,
):
    gx, gy = lax.axis_index("gx"), lax.axis_index("gy")
    y, zh, c = gx // 8, (gx // 2) % 4, gx % 2
    x, zl = gy // 4, gy % 4

    def at(y_, zh_, c_):
        return (y_ % 4) * 8 + (zh_ % 4) * 2 + c_

    def other(x_, zl_):
        return (x_ % 4) * 4 + zl_ % 4

    zpeer = [(at(y, zh + d, c), gy) for d in (1, 2, 3)]
    ypeer = [(at(y + d, zh, c), gy) for d in (1, 2, 3)]
    cpeer = (at(y, zh, 1 - c), gy)
    lpeer = [(gx, other(x, zl + d)) for d in (1, 2, 3)]
    xpeer = [(gx, other(x + d, zl)) for d in (1, 2, 3)]
    hx = [((gx + 31) % 32, gy), ((gx + 1) % 32, gy)]
    hy = [(gx, (gy + 15) % 16), (gx, (gy + 1) % 16)]

    barrier = pltpu.get_barrier_semaphore()
    everyone = zpeer + ypeer + [cpeer] + lpeer + xpeer + hx + hy
    for peer in everyone:
        pl.semaphore_signal(barrier, inc=1, device_id=peer, device_id_type=MESH)

    loads = [
        pltpu.make_async_copy(a, b, lsem.at[i])
        for i, (a, b) in enumerate(
            [
                (core, core_v), (pres, pres_v), (prev, prev_v), (vel, vel_v), (f1, f1_v), (pf1, pf1_v),
                (f2, f2_v), (pf2, pf2_v), (dep, dep_v), (down, down_v), (across, across_v),
            ]
        )
    ]
    for load in loads:
        load.start()

    def remote(src, dst, ssem, rsem, peer):
        return pltpu.make_async_remote_copy(
            src_ref=src, dst_ref=dst, send_sem=ssem, recv_sem=rsem, device_id=peer, device_id_type=MESH
        )

    sent = []

    def send(src, dst, ssem, rsem, peer):
        copy = remote(src, dst, ssem, rsem, peer)
        copy.start()
        sent.append(copy)

    def arrive(dst, ssem, rsem, peer):
        remote(dst, dst, ssem, rsem, peer).wait_recv()

    loads[0].wait()
    for s in range(STEPS):
        raw = core_v[s].astype(F32)
        tail = jnp.concatenate([raw[8:12, :384], raw[8:12, 384:]], axis=0)
        kb[s, c, y, zh] = jnp.concatenate([raw[:8], tail], axis=1).astype(BF16)

    pl.semaphore_wait(barrier, len(everyone))
    for s in range(STEPS):
        for d in range(3):
            own = kb.at[s, c, y, zh]
            send(own, own, zs.at[s, d], zr.at[s, d], zpeer[d])

    def pack_tile(level):
        def run(i, carry):
            for side, row in ((0, 8), (1, 20)):
                hxs[level, side, i, 0:4] = fld[level, 2 + i, row : row + 4]
                hxs[level, side, i, 4:8] = fld[level, 2 + TILES // 2 + i, row : row + 4]
            return carry

        lax.fori_loop(0, TILES // 2, run, 0, unroll=4)
        hys[level, 0] = fld[level, 2:4, 8:24]
        hys[level, 1] = fld[level, TILES : TILES + 2, 8:24]

    def send_halo(level):
        pack_tile(level)
        for side in (1, 0):
            send(hxs.at[level, side], hxr.at[level, 1 - side], hxss.at[level, side], hxrs.at[level, 1 - side], hx[side])
            send(hys.at[level, side], hyr.at[level, 1 - side], hyss.at[level, side], hyrs.at[level, 1 - side], hy[side])

    loads[1].wait()

    def spread(i, carry):
        fld[0, 2 + i, 8:24] = pres_v[:, pl.ds(pl.multiple_of(i * 128, 128), 128)]
        return carry

    lax.fori_loop(0, TILES, spread, 0, unroll=4)
    send_halo(0)

    for load in loads[4:]:
        load.wait()
    f1p = dot(f1_v[...], pf1_v[...]).astype(BF16)
    f1a_s[...] = f1p[:, :256]
    f1b_s[0:16] = f1p[:, 256:512]
    f1b_s[16:32] = f1p[:, 512:768]
    f2p_s[...] = dot(f2_v[...], pf2_v[...]).astype(BF16)
    tall = lax.dot_general(down_v[...], dep_v[...], (((1,), (1,)), ((), ())), preferred_element_type=F32)
    wide = dot(tall.astype(BF16), across_v[...])
    block_row = lax.broadcasted_iota(jnp.int32, (128, 256), 0) // 32
    block_col = lax.broadcasted_iota(jnp.int32, (128, 256), 1) // 64
    wide = jnp.where(block_row == block_col, wide, 0.0).astype(BF16)
    bd_s[0:128] = wide
    bd_s[128:256] = wide

    lane = lax.broadcasted_iota(jnp.int32, (CX, 128), 1)
    low_half = lane < 64
    level_z = lane % 64
    lane8 = lax.broadcasted_iota(jnp.int32, (8, 128), 1)

    def along_y(s):
        for d in range(3):
            slot = kb.at[s, c, y, (zh + 3 - d) % 4]
            arrive(slot, zs.at[s, d], zr.at[s, d], zpeer[d])
        row = kb.at[s, c, y]
        for d in range(3):
            send(row, row, ys.at[s, d], yr.at[s, d], ypeer[d])
        send(row, row, cs.at[s, 3], cr.at[s, 3], cpeer)

    def to_core(s):
        for d in range(3):
            row = kb.at[s, c, (y + 3 - d) % 4]
            arrive(row, ys.at[s, d], yr.at[s, d], ypeer[d])
            send(row, row, cs.at[s, d], cr.at[s, d], cpeer)

    def partial(s):
        arrive(kb.at[s, 1 - c, y], cs.at[s, 3], cr.at[s, 3], cpeer)
        for d in range(3):
            arrive(kb.at[s, 1 - c, (y + 3 - d) % 4], cs.at[s, d], cr.at[s, d], cpeer)
        blocks = kb[s].reshape(256, 1152)
        top = dot(f1a_s[...], blocks[:, :768])
        low = dot(f1b_s[...], blocks[:, 768:])
        value = top + jnp.concatenate([low[:16], low[16:]], axis=1)
        largest = jnp.max(jnp.abs(value), axis=(0, 1), keepdims=True)
        largest = jnp.maximum(largest * 1.01, 1e-30).astype(BF16).astype(F32)
        code = encode(value, LIFT / largest)
        for q in range(6):
            v_s[16 * q : 16 * q + 16] = code[:, 128 * q : 128 * q + 128]
        v_s[96:128] = jnp.zeros((32, 128), F32)
        rows = [v_s[pl.ds(i, 8, stride=16), :] for i in range(16)]
        for m in range(4):
            for j in range(4):
                chunk = None
                for t in range(4):
                    piece = rows[(t % 2) * 8 + 2 * j + t // 2]
                    shift = (32 * (t - m)) % 128
                    piece = pltpu.roll(piece, shift, 1) if shift else piece
                    chunk = piece if t == 0 else jnp.where(lane8 < 32 * t, chunk, piece)
                w_s[6 * m : 6 * m + 6, 128 * j : 128 * j + 128] = chunk[0:6]
        fold = jnp.concatenate([w_s[16:24, 0:256], w_s[16:24, 256:512]], axis=0)
        mark = jnp.broadcast_to(largest, (16, 128))
        gb[s, x, zl] = jnp.concatenate([w_s[0:16, :], fold, mark], axis=1).astype(BF16)
        own = gb.at[s, x, zl]
        for d in range(3):
            send(own, own, gzs.at[s, d], gzr.at[s, d], lpeer[d])

    def along_x(s):
        for d in range(3):
            arrive(gb.at[s, x, (zl + 3 - d) % 4], gzs.at[s, d], gzr.at[s, d], lpeer[d])
        row = gb.at[s, x]
        for d in range(3):
            send(row, row, gxs.at[s, d], gxr.at[s, d], xpeer[d])

    def step(t):
        for side in range(2):
            arrive(hxr.at[t, side], hxss.at[t, side], hxrs.at[t, side], hx[side])
            arrive(hyr.at[t, side], hyss.at[t, side], hyrs.at[t, side], hy[side])
        open_x = [gx > 0, gx < 31]
        open_y = [gy > 0, gy < 15]
        for side, first in ((0, 0), (1, TILES + 2)):
            fld[t, first : first + 2, 8:24] = jnp.where(open_y[side], hyr[t, side], 0.0)

        def place(i, carry):
            for side, row in ((0, 4), (1, 24)):
                got = jnp.where(open_x[side], hxr[t, side, i], 0.0)
                fld[t, 2 + i, row : row + 4] = got[0:4]
                fld[t, 2 + TILES // 2 + i, row : row + 4] = got[4:8]
            return carry

        lax.fori_loop(0, TILES // 2, place, 0, unroll=4)

        def turn(i, carry):
            rolled[i] = pltpu.roll(fld[t, i, 8:24], 64, 1)
            return carry

        lax.fori_loop(0, TILES + 4, turn, 0, unroll=4)

        def tile(i, carry):
            lanes = pl.ds(pl.multiple_of(i * 128, 128), 128)
            n = i + 2
            v = fld[t, n, 8:24]
            total = 3.0 * STENCIL[0] * v
            along = {
                1: rolled[n] + jnp.where(low_half, rolled[n - 1], rolled[n + 1]),
                2: fld[t, n - 1, 8:24] + fld[t, n + 1, 8:24],
                3: jnp.where(low_half, rolled[n + 1], rolled[n + 2]) + jnp.where(low_half, rolled[n - 2], rolled[n - 1]),
                4: fld[t, n - 2, 8:24] + fld[t, n + 2, 8:24],
            }
            for k in range(1, 5):
                near = along[k] + (fld[t, n, 8 - k : 24 - k] + fld[t, n, 8 + k : 24 + k])
                near = near + jnp.where(level_z + k < NZ, pltpu.roll(v, 128 - k, 1), 0.0)
                near = near + jnp.where(level_z >= k, pltpu.roll(v, k, 1), 0.0)
                total = total + STENCIL[k] * near
            before = prev_v[:, lanes] if t == 0 else fld[t - 1, n, 8:24]
            following = 2.0 * v - before + vel_v[:, lanes].astype(F32) * total
            if t < STEPS - 1:
                fld[t + 1, n, 8:24] = following
            else:
                last[i] = following
            return carry

        lax.fori_loop(0, TILES, tile, 0, unroll=2)
        if t < STEPS - 1:
            send_halo(t + 1)

    def finish(s):
        for d in range(3):
            arrive(gb.at[s, (x + 3 - d) % 4], gxs.at[s, d], gxr.at[s, d], xpeer[d])

        def block(b, carry):
            got = gb[s, b // 4, b % 4].astype(F32)
            scale = got[:, 768:896] * (1.0 / LIFT)
            value = jnp.concatenate(
                [decode(got[:, 128 * q : 128 * q + 128], scale) for q in range(6)], axis=1
            )
            start = pl.multiple_of(b * 24, 8)
            g_s[pl.ds(start, 16), :] = value[:, :512]
            g_s[pl.ds(pl.multiple_of(start + 16, 8), 8), :] = jnp.concatenate(
                [value[0:8, 512:768], value[8:16, 512:768]], axis=1
            )
            return carry

        lax.fori_loop(0, 16, block, 0)
        high, low = halves(g_s[...])
        mixed = dot(f2p_s[...], high) + dot(f2p_s[...], low)
        high, low = halves(mixed)
        for j in range(4):
            cols = slice(128 * j, 128 * j + 128)
            deep = dot(jnp.concatenate([high[:, cols], low[:, cols]], axis=1), bd_s[...])
            t_s[2 * j * YL : (2 * j + 1) * YL] = deep[:, :128]
            t_s[(2 * j + 1) * YL : (2 * j + 2) * YL] = deep[:, 128:]
        half8 = lane8 < 64

        def tile(i, carry):
            lanes = pl.ds(pl.multiple_of(i * 128, 128), 128)
            even = t_s[pl.ds(2 * i, 8, stride=YL), :]
            odd = t_s[pl.ds(2 * i + 1, 8, stride=YL), :]
            upper = jnp.where(half8, even, pltpu.roll(odd, 64, 1))
            lower = jnp.where(half8, pltpu.roll(even, 64, 1), odd)
            if s < STEPS - 1:
                following = fld[s + 1, i + 2, 8:24]
            else:
                following = last[i]
            term = jnp.concatenate([upper, lower], axis=0) * following
            out[:, lanes] = term if s == 0 else out[:, lanes] + term
            return carry

        lax.fori_loop(0, TILES, tile, 0, unroll=4)

    along_y(0)
    along_y(1)
    along_y(2)
    loads[2].wait()
    loads[3].wait()
    to_core(0)
    step(0)
    partial(0)
    to_core(1)
    partial(1)
    to_core(2)
    along_x(0)
    step(1)
    partial(2)
    along_x(1)
    finish(0)
    step(2)
    along_x(2)
    finish(1)
    finish(2)
    for copy in sent:
        copy.wait_send()


def body(pressure, previous, velocity, tucker_core, first_factor, second_factor, depth_factor):
    args = (pressure, previous, velocity, tucker_core, first_factor, second_factor, depth_factor) + constants()
    dma = pltpu.SemaphoreType.DMA
    return pl.pallas_call(
        kernel,
        out_shape=jax.ShapeDtypeStruct(pressure.shape, F32),
        in_specs=[pl.BlockSpec(memory_space=pl.ANY)] * len(args),
        out_specs=pl.BlockSpec(memory_space=pltpu.VMEM),
        scratch_shapes=[
            pltpu.VMEM(a.shape, a.dtype) for a in args
        ]
        + [
            pltpu.VMEM((STEPS, 2, 4, 4, 8, 1152), BF16),
            pltpu.VMEM((STEPS, 4, 4, 16, 896), BF16),
            pltpu.VMEM((STEPS, TILES + 4, 32, 128), F32),
            pltpu.VMEM((TILES + 4, CX, 128), F32),
            pltpu.VMEM((TILES, CX, 128), F32),
            pltpu.VMEM((STEPS, 2, TILES // 2, 8, 128), F32),
            pltpu.VMEM((STEPS, 2, TILES // 2, 8, 128), F32),
            pltpu.VMEM((STEPS, 2, 2, CX, 128), F32),
            pltpu.VMEM((STEPS, 2, 2, CX, 128), F32),
            pltpu.VMEM((128, 128), F32),
            pltpu.VMEM((24, 512), F32),
            pltpu.VMEM((384, 512), F32),
            pltpu.VMEM((8 * YL, 128), F32),
            pltpu.VMEM((256, 256), BF16),
            pltpu.VMEM((16, 256), BF16),
            pltpu.VMEM((32, 256), BF16),
            pltpu.VMEM((YL, 384), BF16),
            dma((len(args),)),
            dma((STEPS, 3)), dma((STEPS, 3)),
            dma((STEPS, 3)), dma((STEPS, 3)),
            dma((STEPS, 4)), dma((STEPS, 4)),
            dma((STEPS, 3)), dma((STEPS, 3)),
            dma((STEPS, 3)), dma((STEPS, 3)),
            dma((STEPS, 2)), dma((STEPS, 2)),
            dma((STEPS, 2)), dma((STEPS, 2)),
        ],
        compiler_params=pltpu.CompilerParams(
            collective_id=0, has_side_effects=True, vmem_limit_bytes=40 << 20
        ),
        name="image_steps",
    )(*args)


def solution(mesh):
    placed = (
        P("gx", "gy"),
        P("gx", "gy"),
        P("gx", "gy"),
        P(None, "gx", "gy"),
        P("gx", None),
        P("gy", None),
        P(),
    )
    return jax.shard_map(body, mesh=mesh, in_specs=placed, out_specs=P("gx", "gy"), check_vma=False)
```

```python
import functools

import jax
import jax.numpy as jnp
import numpy as np
from jax import lax
from jax.experimental import pallas as pl
from jax.experimental.pallas import tpu as pltpu
from jax.sharding import PartitionSpec as P

STENCIL = (-205.0 / 72.0, 8.0 / 5.0, -1.0 / 5.0, 8.0 / 315.0, -1.0 / 560.0)
MESH = pl.DeviceIdType.MESH
F32, BF16 = jnp.float32, jnp.bfloat16

STEPS = 3
CX = 16
NZ = 64
YL = 96
TILES = YL * NZ // 128
POWER = 13.0
LIFT = 512.0


def constants():
    first = np.zeros((384, 768), np.float32)
    for core in range(2):
        for y in range(4):
            for zh in range(4):
                block = (y * 4 + zh) * 2 + core
                slot = (core * 4 + y) * 4 + zh
                for r in range(8):
                    first[block * 12 + r, slot * 8 + r] = 1.0
                for r in range(4):
                    first[block * 12 + 8 + r, 256 + slot * 8 + r] = 1.0
                    first[block * 12 + 8 + r, 512 + slot * 8 + 4 + r] = 1.0
    second = np.zeros((384, 384), np.float32)
    for block in range(16):
        for m in range(4):
            for q in range(6):
                second[block * 24 + 4 * q + m, block * 24 + 6 * m + q] = 1.0
    down = np.tile(np.eye(32, dtype=np.float32), (4, 1))
    across = np.tile(np.eye(64, dtype=np.float32), (1, 4))
    z = np.arange(128)
    lines = np.zeros((128, 128), np.float64)
    for k in range(1, 5):
        near = np.abs(z[:, None] - z[None, :]) == k
        lines += STENCIL[k] * (near & (z[:, None] // 64 == z[None, :] // 64))
    swap = (np.abs(z[:, None] - z[None, :]) == 64).astype(np.float64)
    lines += STENCIL[1] * swap
    high = lines.astype(BF16)
    low = (lines - high.astype(np.float64)).astype(BF16)
    top = np.concatenate([high, swap.astype(BF16)], axis=1)
    near_z = np.concatenate([top, top, np.concatenate([low, np.zeros((128, 128), BF16)], axis=1)], axis=0)
    return tuple(jnp.asarray(a, BF16) for a in (first, second, down, across, near_z))


def dot(a, b):
    return lax.dot_general(a, b, (((1,), (0,)), ((), ())), preferred_element_type=F32)


def halves(a):
    high = a.astype(BF16)
    return high, (a - high.astype(F32)).astype(BF16)


def encode(value, scale):
    u = value * scale
    u2 = u * u
    u4 = u2 * u2
    return u4 * u4 * u4 * u


def decode(code, scale):
    size = jnp.abs(code)
    root = jnp.exp2(jnp.log2(jnp.maximum(size, 1e-38)) * (1.0 / POWER)) * scale
    root = jnp.where(size < 1e-37, 0.0, root)
    return jnp.where(code < 0.0, -root, root)


def place(x, r):
    return ((x + 4) * 10 + r + 2) * 8


def kernel(
    pres, prev, vel, core, f1, f2, dep, pf1, pf2, down, across, near_z,
    out,
    pres_v, prev_v, vel_v, core_v, f1_v, f2_v, dep_v, pf1_v, pf2_v, down_v, across_v, near_z_v,
    kb, gb, fld, swapped, deep_z, speed, last, image, hxs, hxr, hys, hyr, v_s, w_s, g_s, t_s, bd_s, f1a_s, f1b_s, f2p_s,
    lsem, zs, zr, ys, yr, cs, cr, gzs, gzr, gxs, gxr, hxss, hxrs, hyss, hyrs,
):
    gx, gy = lax.axis_index("gx"), lax.axis_index("gy")
    y, zh, c = gx // 8, (gx // 2) % 4, gx % 2
    x, zl = gy // 4, gy % 4

    def at(y_, zh_, c_):
        return ((y_ % 4) * 8 + (zh_ % 4) * 2 + c_, gy)

    def other(x_, zl_):
        return (gx, (x_ % 4) * 4 + zl_ % 4)

    zpeer = [at(y, zh + d, c) for d in (1, 2, 3)]
    ypeer = [at(y + d, zh, c) for d in (1, 2, 3)]
    cpeer = at(y, zh, 1 - c)
    lpeer = [other(x, zl + d) for d in (1, 2, 3)]
    xpeer = [other(x + 1, zl), other(x + 3, zl)]
    hx = [((gx + 31) % 32, gy), ((gx + 1) % 32, gy)]
    hy = [(gx, (gy + 15) % 16), (gx, (gy + 1) % 16)]

    barrier = pltpu.get_barrier_semaphore()
    everyone = zpeer + ypeer + [cpeer] + lpeer + xpeer + hx + hy
    for peer in everyone:
        pl.semaphore_signal(barrier, inc=1, device_id=peer, device_id_type=MESH)

    loads = [
        pltpu.make_async_copy(a, b, lsem.at[i])
        for i, (a, b) in enumerate(
            [
                (core, core_v), (pres, pres_v), (prev, prev_v), (vel, vel_v), (f1, f1_v), (pf1, pf1_v),
                (f2, f2_v), (pf2, pf2_v), (dep, dep_v), (down, down_v), (across, across_v), (near_z, near_z_v),
            ]
        )
    ]
    for load in loads:
        load.start()

    def remote(src, dst, ssem, rsem, peer):
        return pltpu.make_async_remote_copy(
            src_ref=src, dst_ref=dst, send_sem=ssem, recv_sem=rsem, device_id=peer, device_id_type=MESH
        )

    sent = []

    def send(src, dst, ssem, rsem, peer):
        copy = remote(src, dst, ssem, rsem, peer)
        copy.start()
        sent.append(copy)

    def arrive(dst, ssem, rsem, peer):
        remote(dst, dst, ssem, rsem, peer).wait_recv()

    def flush(count=None):
        for _ in range(len(sent) if count is None else count):
            sent.pop(0).wait_send()

    loads[0].wait()
    for s in range(STEPS):
        raw = core_v[s].astype(F32)
        tail = jnp.concatenate([raw[8:12, :384], raw[8:12, 384:]], axis=0)
        kb[s, c, y, zh] = jnp.concatenate([raw[:8], tail], axis=1).astype(BF16)

    def along_z(s):
        own = kb.at[s, c, y, zh]
        for k in range(3):
            to = k + jnp.where(k >= zh, 1, 0)
            send(own, own, zs.at[s, k], zr.at[s, zh], at(y, to, c))

    def along_y(s):
        for d in range(3):
            source = (zh + 3 - d) % 4
            arrive(kb.at[s, c, y, source], zs.at[s, d], zr.at[s, source], zpeer[d])
        row = kb.at[s, c, y]
        for d in (0, 2, 1):
            send(row, row, ys.at[s, d], yr.at[s, d], ypeer[d])
        send(row, row, cs.at[s, 3], cr.at[s, 3], cpeer)

    def to_core(s):
        for d in (0, 2, 1):
            row = kb.at[s, c, (y + 3 - d) % 4]
            arrive(row, ys.at[s, d], yr.at[s, d], ypeer[d])
            send(row, row, cs.at[s, d], cr.at[s, d], cpeer)

    low_half = lax.broadcasted_iota(jnp.int32, (8, 128), 1) < 64
    sub = lax.broadcasted_iota(jnp.int32, (8, 128), 0)

    def rows(start, count=8):
        return pl.ds(pl.multiple_of(start, 8), count)

    def strided(x_, r):
        return pl.ds((x_ // 8) * 384 + r * 8 + x_ % 8, 8, stride=48)

    def send_halo(t):
        for side in range(2):
            for k in range(4):
                layer = k if side == 0 else 12 + k
                outer = k == 0 if side == 0 else k == 3
                for p in range(3):
                    pair = fld[t, rows(place(layer, 2 * p), 16), :]
                    high = pair.astype(BF16)
                    hxs[t, side, k, p] = high
                    if outer:
                        hxs[t, side, 4, p] = (pair - high.astype(F32)).astype(BF16)
        for side in range(2):
            for i in range(2):
                for half in range(2):
                    start = place(8 * half, i) if side == 0 else place(8 * half, 4 + i) + 7
                    hys[t, side, i, 8 * half : 8 * half + 8] = fld[t, pl.ds(start, 8, stride=80), :]
        for side in (1, 0):
            send(hxs.at[t, side], hxr.at[t, 1 - side], hxss.at[t, side], hxrs.at[t, 1 - side], hx[side])
            send(hys.at[t, side], hyr.at[t, 1 - side], hyss.at[t, side], hyrs.at[t, 1 - side], hy[side])

    def inner(t):
        def run(q, carry):
            cells = jnp.concatenate([fld[t, rows(place(4 * q + k, 0), 48), :] for k in range(4)], axis=0)
            high, low = halves(cells)
            both = dot(jnp.concatenate([high, low], axis=1), near_z_v[0:256])
            along = both[:, :128] + dot(high, near_z_v[256:384, :128])
            for k in range(4):
                deep_z[rows((4 * q + k) * 48, 48), :] = along[48 * k : 48 * k + 48]
                swapped[rows(place(4 * q + k, 0), 48), :] = both[48 * k : 48 * k + 48, 128:]
            return carry

        lax.fori_loop(0, 4, run, 0)

    def step(t):
        for side in range(2):
            arrive(hyr.at[t, side], hyss.at[t, side], hyrs.at[t, side], hy[side])
        open_y = [gy > 0, gy < 15]
        edges = ((-2, 4, 0, 0, 1), (-1, 5, 0, 1, 1), (6, 0, 1, 0, 7), (7, 1, 1, 1, 7))
        for _, _, side, i, _ in edges:
            hyr[t, side, i] = jnp.where(open_y[side], hyr[t, side, i], 0.0)

        def edge(x_, carry):
            for r, source, side, i, turn in edges:
                halo = hyr[t, side, i, pl.ds(x_, 1), :]
                here = sub == (0 if side == 0 else 7)
                moved = pltpu.roll(fld[t, rows(place(x_, source)), :], turn, 0)
                fld[t, rows(place(x_, r)), :] = jnp.where(here, halo, moved)
                moved = pltpu.roll(swapped[rows(place(x_, source)), :], turn, 0)
                swapped[rows(place(x_, r)), :] = jnp.where(here, pltpu.roll(halo, 64, 1), moved)
            return carry

        lax.fori_loop(0, CX, edge, 0, unroll=2)
        for side in range(2):
            arrive(hxr.at[t, side], hxss.at[t, side], hxrs.at[t, side], hx[side])
        open_x = [gx > 0, gx < 31]
        for side in range(2):
            for k in range(4):
                layer = k - 4 if side == 0 else 16 + k
                outer = k == 3 if side == 0 else k == 0
                for p in range(3):
                    pair = hxr[t, side, k, p].astype(F32)
                    if outer:
                        pair = pair + hxr[t, side, 4, p].astype(F32)
                    fld[t, rows(place(layer, 2 * p), 16), :] = jnp.where(open_x[side], pair, 0.0)

        def line(x_, carry):
            v = {r: fld[t, rows(place(x_, r)), :] for r in range(-2, 8)}
            w = {r: swapped[rows(place(x_, r)), :] for r in range(-2, 8)}
            for r in range(6):
                along = {
                    1: jnp.where(low_half, w[r - 1], w[r + 1]),
                    2: v[r - 1] + v[r + 1],
                    3: jnp.where(low_half, w[r + 1], w[r + 2]) + jnp.where(low_half, w[r - 2], w[r - 1]),
                    4: v[r - 2] + v[r + 2],
                }
                total = deep_z[rows((x_ * 6 + r) * 8), :] + (3.0 * STENCIL[0]) * v[r]
                for k in range(1, 5):
                    near = fld[t, rows(place(x_ - k, r)), :] + fld[t, rows(place(x_ + k, r)), :]
                    total = total + STENCIL[k] * (near + along[k])
                if t == 0:
                    before = prev_v[strided(x_, r), :]
                else:
                    before = fld[t - 1, rows(place(x_, r)), :]
                following = 2.0 * v[r] - before + speed[rows((x_ * 6 + r) * 8), :] * total
                if t < STEPS - 1:
                    fld[t + 1, rows(place(x_, r)), :] = following
                else:
                    last[rows((x_ * 6 + r) * 8), :] = following
            return carry

        lax.fori_loop(0, CX, line, 0)
        if t < STEPS - 1:
            send_halo(t + 1)
            inner(t + 1)

    lane8 = lax.broadcasted_iota(jnp.int32, (8, 128), 1)

    def partial(s):
        arrive(kb.at[s, 1 - c, y], cs.at[s, 3], cr.at[s, 3], cpeer)
        for d in range(3):
            arrive(kb.at[s, 1 - c, (y + 3 - d) % 4], cs.at[s, d], cr.at[s, d], cpeer)
        blocks = kb[s].reshape(256, 1152)
        top = dot(f1a_s[...], blocks[:, :768])
        low = dot(f1b_s[...], blocks[:, 768:])
        value = top + jnp.concatenate([low[:16], low[16:]], axis=1)
        largest = jnp.max(jnp.abs(value), axis=(0, 1), keepdims=True)
        largest = jnp.maximum(largest * 1.01, 1e-30).astype(BF16).astype(F32)
        code = encode(value, LIFT / largest)
        for q in range(6):
            v_s[16 * q : 16 * q + 16] = code[:, 128 * q : 128 * q + 128]
        v_s[96:128] = jnp.zeros((32, 128), F32)
        lines = [v_s[pl.ds(i, 8, stride=16), :] for i in range(16)]
        for m in range(4):
            for j in range(4):
                chunk = None
                for t in range(4):
                    piece = lines[(t % 2) * 8 + 2 * j + t // 2]
                    shift = (32 * (t - m)) % 128
                    piece = pltpu.roll(piece, shift, 1) if shift else piece
                    chunk = piece if t == 0 else jnp.where(lane8 < 32 * t, chunk, piece)
                w_s[6 * m : 6 * m + 6, 128 * j : 128 * j + 128] = chunk[0:6]
        fold = jnp.concatenate([w_s[16:24, 0:256], w_s[16:24, 256:512]], axis=0)
        mark = jnp.broadcast_to(largest, (16, 128))
        gb[s, x, zl] = jnp.concatenate([w_s[0:16, :], fold, mark], axis=1).astype(BF16)
        own = gb.at[s, x, zl]
        for d in range(3):
            send(own, own, gzs.at[s, d], gzr.at[s, d], lpeer[d])

    def decode_row(s, row):
        def block(b, carry):
            got = gb[s, row, b].astype(F32)
            scale = got[:, 768:896] * (1.0 / LIFT)
            value = jnp.concatenate([decode(got[:, 128 * q : 128 * q + 128], scale) for q in range(6)], axis=1)
            start = (row * 4 + b) * 24
            g_s[s, rows(start, 16), :] = value[:, :512]
            g_s[s, rows(start + 16), :] = jnp.concatenate([value[0:8, 512:768], value[8:16, 512:768]], axis=1)
            return carry

        lax.fori_loop(0, 4, block, 0)

    def start_x(s):
        for d in range(3):
            arrive(gb.at[s, x, (zl + 3 - d) % 4], gzs.at[s, d], gzr.at[s, d], lpeer[d])
        row = gb.at[s, x]
        for side in range(2):
            send(row, row, gxs.at[s, side], gxr.at[s, side], xpeer[side])
        decode_row(s, x)

    def forward_x(s):
        for side in range(2):
            source = (x + 3 - 2 * side) % 4
            arrive(gb.at[s, source], gxs.at[s, side], gxr.at[s, side], xpeer[side])
            half = gb.at[s, source, pl.ds(2 * side, 2)]
            send(half, half, gxs.at[s, 2 + side], gxr.at[s, 2 + side], xpeer[side])
        for side in range(2):
            decode_row(s, (x + 3 - 2 * side) % 4)

    def finish(s):
        for side in range(2):
            half = gb.at[s, (x + 2) % 4, pl.ds(2 * side, 2)]
            arrive(half, gxs.at[s, 2 + side], gxr.at[s, 2 + side], xpeer[side])
        decode_row(s, (x + 2) % 4)
        high, low = halves(g_s[s])
        mixed = dot(f2p_s[...], high) + dot(f2p_s[...], low)
        high, low = halves(mixed)
        for j in range(4):
            cols = slice(128 * j, 128 * j + 128)
            deep = dot(jnp.concatenate([high[:, cols], low[:, cols]], axis=1), bd_s[...])
            for i in range(4):
                start = (i // 2) * 8 * YL + (2 * j + i % 2) * YL
                t_s[start : start + YL] = deep[:, 128 * i : 128 * i + 128]

        def line(j, carry):
            for r in range(6):
                even, odd, even_turned, odd_turned = (
                    t_s[pl.ds(j * YL + 2 * r + offset, 8, stride=12), :] for offset in (0, 1, 8 * YL, 8 * YL + 1)
                )
                for x2, term in (
                    (0, jnp.where(low_half, even, odd_turned)),
                    (1, jnp.where(low_half, even_turned, odd)),
                ):
                    x_ = x2 * 8 + j
                    here = rows((x_ * 6 + r) * 8)
                    if s < STEPS - 1:
                        term = term * fld[s + 1, rows(place(x_, r)), :]
                    else:
                        term = term * last[here, :]
                    if s > 0:
                        term = term + image[here, :]
                    if s < STEPS - 1:
                        image[here, :] = term
                    else:
                        out[strided(x_, r), :] = term
            return carry

        lax.fori_loop(0, 8, line, 0)

    def prepare():
        for load in loads[4:11]:
            load.wait()
        f1p = dot(f1_v[...], pf1_v[...]).astype(BF16)
        f1a_s[...] = f1p[:, :256]
        f1b_s[0:16] = f1p[:, 256:512]
        f1b_s[16:32] = f1p[:, 512:768]
        f2p_s[...] = dot(f2_v[...], pf2_v[...]).astype(BF16)
        tall = dot(down_v[...], dep_v[...])
        wide = dot(tall.astype(BF16), across_v[...])
        block_row = lax.broadcasted_iota(jnp.int32, (128, 256), 0) // 32
        block_col = lax.broadcasted_iota(jnp.int32, (128, 256), 1) // 64
        swap_col = block_col + 1 - 2 * (block_col % 2)
        for i, col in enumerate((block_col, swap_col)):
            part = jnp.where(block_row == col, wide, 0.0).astype(BF16)
            bd_s[0:128, 256 * i : 256 * i + 256] = part
            bd_s[128:256, 256 * i : 256 * i + 256] = part

    def first_fields():
        loads[1].wait()

        def spread(xs, carry):
            for xt in range(2):
                for r in range(6):
                    fld[0, rows(place(xt * 8 + xs, r)), :] = pres_v[pl.ds(xt * 384 + r * 8 + xs, 8, stride=48), :]
            return carry

        lax.fori_loop(0, 8, spread, 0)

    def speeds():
        loads[3].wait()
        last[...] = vel_v[...].astype(F32)

        def spread(xs, carry):
            for xt in range(2):
                for r in range(6):
                    speed[rows(((xt * 8 + xs) * 6 + r) * 8), :] = last[pl.ds(xt * 384 + r * 8 + xs, 8, stride=48), :]
            return carry

        lax.fori_loop(0, 8, spread, 0)
        loads[2].wait()

    pl.semaphore_wait(barrier, len(everyone))
    along_z(0)
    first_fields()
    send_halo(0)
    flush(3)
    along_z(1)
    prepare()
    loads[11].wait()
    inner(0)
    flush(4)
    flush(3)
    along_z(2)
    speeds()
    along_y(0)
    along_y(1)
    to_core(0)
    step(0)
    along_y(2)
    partial(0)
    to_core(1)
    partial(1)
    start_x(0)
    to_core(2)
    partial(2)
    start_x(1)
    forward_x(0)
    step(1)
    start_x(2)
    forward_x(1)
    finish(0)
    forward_x(2)
    step(2)
    finish(1)
    finish(2)
    flush()


def tiles(a):
    return a.reshape(2, 8, TILES, 128).transpose(0, 2, 1, 3).reshape(CX * TILES, 128)


def body(pressure, previous, velocity, tucker_core, first_factor, second_factor, depth_factor):
    args = (tiles(pressure), tiles(previous), tiles(velocity), tucker_core, first_factor, second_factor, depth_factor.T)
    args = args + constants()
    dma = pltpu.SemaphoreType.DMA
    image = pl.pallas_call(
        kernel,
        out_shape=jax.ShapeDtypeStruct((CX * TILES, 128), F32),
        in_specs=[pl.BlockSpec(memory_space=pl.ANY)] * len(args),
        out_specs=pl.BlockSpec(memory_space=pltpu.VMEM),
        scratch_shapes=[
            pltpu.VMEM(a.shape, a.dtype) for a in args
        ]
        + [
            pltpu.VMEM((STEPS, 2, 4, 4, 8, 1152), BF16),
            pltpu.VMEM((STEPS, 4, 4, 16, 896), BF16),
            pltpu.VMEM((STEPS, 24 * 10 * 8, 128), F32),
            pltpu.VMEM((24 * 10 * 8, 128), F32),
            pltpu.VMEM((CX * TILES, 128), F32),
            pltpu.VMEM((CX * TILES, 128), F32),
            pltpu.VMEM((CX * TILES, 128), F32),
            pltpu.VMEM((CX * TILES, 128), F32),
            pltpu.VMEM((STEPS, 2, 5, 3, 16, 128), BF16),
            pltpu.VMEM((STEPS, 2, 5, 3, 16, 128), BF16),
            pltpu.VMEM((STEPS, 2, 2, CX, 128), F32),
            pltpu.VMEM((STEPS, 2, 2, CX, 128), F32),
            pltpu.VMEM((128, 128), F32),
            pltpu.VMEM((24, 512), F32),
            pltpu.VMEM((STEPS, 384, 512), F32),
            pltpu.VMEM((2 * 8 * YL, 128), F32),
            pltpu.VMEM((256, 512), BF16),
            pltpu.VMEM((16, 256), BF16),
            pltpu.VMEM((32, 256), BF16),
            pltpu.VMEM((YL, 384), BF16),
            dma((len(args),)),
            dma((STEPS, 3)), dma((STEPS, 4)),
            dma((STEPS, 3)), dma((STEPS, 3)),
            dma((STEPS, 4)), dma((STEPS, 4)),
            dma((STEPS, 3)), dma((STEPS, 3)),
            dma((STEPS, 4)), dma((STEPS, 4)),
            dma((STEPS, 2)), dma((STEPS, 2)),
            dma((STEPS, 2)), dma((STEPS, 2)),
        ],
        compiler_params=pltpu.CompilerParams(
            collective_id=0, has_side_effects=True, vmem_limit_bytes=60 << 20
        ),
        name="image_steps",
    )(*args)
    return image.reshape(2, TILES, 8, 128).transpose(0, 2, 1, 3).reshape(CX, 8 * TILES * 16)


def solution(mesh):
    placed = (
        P("gx", "gy"),
        P("gx", "gy"),
        P("gx", "gy"),
        P(None, "gx", "gy"),
        P("gx", None),
        P("gy", None),
        P(),
    )
    return jax.shard_map(body, mesh=mesh, in_specs=placed, out_specs=P("gx", "gy"), check_vma=False)
```

```python
import functools

import jax
import jax.numpy as jnp
import numpy as np
from jax import lax
from jax.experimental import pallas as pl
from jax.experimental.pallas import tpu as pltpu
from jax.sharding import PartitionSpec as P

STENCIL = (-205.0 / 72.0, 8.0 / 5.0, -1.0 / 5.0, 8.0 / 315.0, -1.0 / 560.0)
MESH = pl.DeviceIdType.MESH
F32, BF16 = jnp.float32, jnp.bfloat16

STEPS = 3
CX = 16
NZ = 64
YL = 96
TILES = YL * NZ // 128
POWER = 13.0
LIFT = 512.0


def constants():
    first = np.zeros((2, 384, 384), np.float32)
    for core in range(2):
        for slot in range(16):
            block = slot * 2 + core
            for r in range(8):
                first[core, block * 12 + r, slot * 8 + r] = 1.0
            for r in range(4):
                first[core, block * 12 + 8 + r, 128 + slot * 8 + r] = 1.0
                first[core, block * 12 + 8 + r, 256 + slot * 8 + 4 + r] = 1.0
    second = np.zeros((384, 384), np.float32)
    for block in range(16):
        for m in range(4):
            for q in range(6):
                second[block * 24 + 4 * q + m, block * 24 + 6 * m + q] = 1.0
    down = np.tile(np.eye(32, dtype=np.float32), (4, 1))
    across = np.tile(np.eye(64, dtype=np.float32), (1, 4))
    z = np.arange(128)
    lines = np.zeros((128, 128), np.float64)
    for k in range(1, 5):
        near = np.abs(z[:, None] - z[None, :]) == k
        lines += STENCIL[k] * (near & (z[:, None] // 64 == z[None, :] // 64))
    swap = (np.abs(z[:, None] - z[None, :]) == 64).astype(np.float64)
    lines += STENCIL[1] * swap
    high = lines.astype(BF16)
    low = (lines - high.astype(np.float64)).astype(BF16)
    top = np.concatenate([high, swap.astype(BF16)], axis=1)
    near_z = np.concatenate([top, top, np.concatenate([low, np.zeros((128, 128), BF16)], axis=1)], axis=0)
    return tuple(jnp.asarray(a, BF16) for a in (first, second, down, across, near_z))


def dot(a, b):
    return lax.dot_general(a, b, (((1,), (0,)), ((), ())), preferred_element_type=F32)


def halves(a):
    high = a.astype(BF16)
    return high, (a - high.astype(F32)).astype(BF16)


def encode(value, scale):
    u = value * scale
    u2 = u * u
    u4 = u2 * u2
    return u4 * u4 * u4 * u


def decode(code, scale):
    size = jnp.abs(code)
    root = jnp.exp2(jnp.log2(jnp.maximum(size, 1e-38)) * (1.0 / POWER)) * scale
    root = jnp.where(size < 1e-37, 0.0, root)
    return jnp.where(code < 0.0, -root, root)


def place(x, r):
    return ((x + 4) * 10 + r + 2) * 8


def kernel(
    pres, prev, vel, core, f1, f2, dep, pf1, pf2, down, across, near_z,
    out,
    pres_v, prev_v, vel_v, core_v, f1_v, f2_v, dep_v, pf1_v, pf2_v, down_v, across_v, near_z_v,
    kb, gb, fld, swapped, deep_z, speed, last, image, hxs, hxr, hys, hyr, v_s, w_s, g_s, t_s, bd_s, f1a_s, f1b_s, f2p_s, f1_r, mine, theirs, got_s,
    lsem, zs, zr, ys, yr, cs, cr, gzs, gzr, gxs, gxr, hxss, hxrs, hyss, hyrs,
):
    gx, gy = lax.axis_index("gx"), lax.axis_index("gy")
    y, zh, c = gx // 8, (gx // 2) % 4, gx % 2
    x, zl = gy // 4, gy % 4

    def at(y_, zh_, c_):
        return ((y_ % 4) * 8 + (zh_ % 4) * 2 + c_, gy)

    def other(x_, zl_):
        return (gx, (x_ % 4) * 4 + zl_ % 4)

    zpeer = [at(y, zh + d, c) for d in (1, 2, 3)]
    ypeer = [at(y + d, zh, c) for d in (1, 2, 3)]
    cpeer = at(y, zh, 1 - c)
    lpeer = [other(x, zl + d) for d in (1, 2, 3)]
    xpeer = [other(x + d, zl) for d in (1, 2, 3)]
    hx = [((gx + 31) % 32, gy), ((gx + 1) % 32, gy)]
    hy = [(gx, (gy + 15) % 16), (gx, (gy + 1) % 16)]

    barrier = pltpu.get_barrier_semaphore()
    everyone = zpeer + ypeer + [cpeer] + lpeer + xpeer + hx + hy
    for peer in everyone:
        pl.semaphore_signal(barrier, inc=1, device_id=peer, device_id_type=MESH)

    loads = [
        pltpu.make_async_copy(a, b, lsem.at[i])
        for i, (a, b) in enumerate(
            [
                (core, core_v), (pres, pres_v), (prev, prev_v), (vel, vel_v), (f1, f1_v), (pf1, pf1_v),
                (f2, f2_v), (pf2, pf2_v), (dep, dep_v), (down, down_v), (across, across_v), (near_z, near_z_v),
            ]
        )
    ]
    for load in loads:
        load.start()

    def remote(src, dst, ssem, rsem, peer):
        return pltpu.make_async_remote_copy(
            src_ref=src, dst_ref=dst, send_sem=ssem, recv_sem=rsem, device_id=peer, device_id_type=MESH
        )

    sent = []

    def send(src, dst, ssem, rsem, peer):
        copy = remote(src, dst, ssem, rsem, peer)
        copy.start()
        sent.append(copy)

    def arrive(dst, ssem, rsem, peer):
        remote(dst, dst, ssem, rsem, peer).wait_recv()

    def flush(count=None):
        for _ in range(len(sent) if count is None else count):
            sent.pop(0).wait_send()

    loads[0].wait()
    for s in range(STEPS):
        raw = core_v[s].astype(F32)
        tail = jnp.concatenate([raw[8:12, :384], raw[8:12, 384:]], axis=0)
        kb[s, y, zh] = jnp.concatenate([raw[:8], tail], axis=1).astype(BF16)
    def along_z(s, k):
        own = kb.at[s, y, zh]
        to = k + jnp.where(k >= zh, 1, 0)
        send(own, own, zs.at[s, k], zr.at[s, zh], at(y, to, c))

    def start_y(s):
        for d in range(3):
            source = (zh + 3 - d) % 4
            arrive(kb.at[s, y, source], zs.at[s, d], zr.at[s, source], zpeer[d])
        row = kb.at[s, y]
        for d in (0, 2, 1):
            send(row, row, ys.at[s, d], yr.at[s, d], ypeer[d])

    def end_y(s):
        for d in range(3):
            arrive(kb.at[s, (y + 3 - d) % 4], ys.at[s, d], yr.at[s, d], ypeer[d])


    low_half = lax.broadcasted_iota(jnp.int32, (8, 128), 1) < 64
    sub = lax.broadcasted_iota(jnp.int32, (8, 128), 0)

    def rows(start, count=8):
        return pl.ds(pl.multiple_of(start, 8), count)

    def strided(x_, r):
        return pl.ds((x_ // 8) * 384 + r * 8 + x_ % 8, 8, stride=48)

    def send_halo(t):
        for side in range(2):
            for k in range(4):
                layer = k if side == 0 else 12 + k
                outer = k == 0 if side == 0 else k == 3
                for p in range(3):
                    pair = fld[t, rows(place(layer, 2 * p), 16), :]
                    high = pair.astype(BF16)
                    hxs[t, side, k, p] = high
                    if outer:
                        hxs[t, side, 4, p] = (pair - high.astype(F32)).astype(BF16)
        for side in range(2):
            for i in range(2):
                for half in range(2):
                    start = place(8 * half, i) if side == 0 else place(8 * half, 4 + i) + 7
                    hys[t, side, i, 8 * half : 8 * half + 8] = fld[t, pl.ds(start, 8, stride=80), :]
        for side in (1, 0):
            send(hxs.at[t, side], hxr.at[t, 1 - side], hxss.at[t, side], hxrs.at[t, 1 - side], hx[side])
            send(hys.at[t, side], hyr.at[t, 1 - side], hyss.at[t, side], hyrs.at[t, 1 - side], hy[side])

    def inner(t):
        def run(q, carry):
            cells = jnp.concatenate([fld[t, rows(place(4 * q + k, 0), 48), :] for k in range(4)], axis=0)
            high, low = halves(cells)
            both = dot(jnp.concatenate([high, low], axis=1), near_z_v[0:256])
            along = both[:, :128] + dot(high, near_z_v[256:384, :128])
            for k in range(4):
                deep_z[rows((4 * q + k) * 48, 48), :] = along[48 * k : 48 * k + 48]
                swapped[rows(place(4 * q + k, 0), 48), :] = both[48 * k : 48 * k + 48, 128:]
            return carry

        lax.fori_loop(0, 4, run, 0)

    def step(t):
        for side in range(2):
            arrive(hyr.at[t, side], hyss.at[t, side], hyrs.at[t, side], hy[side])
        open_y = [gy > 0, gy < 15]
        edges = ((-2, 4, 0, 0, 1), (-1, 5, 0, 1, 1), (6, 0, 1, 0, 7), (7, 1, 1, 1, 7))
        for _, _, side, i, _ in edges:
            hyr[t, side, i] = jnp.where(open_y[side], hyr[t, side, i], 0.0)

        def edge(x_, carry):
            for r, source, side, i, turn in edges:
                halo = hyr[t, side, i, pl.ds(x_, 1), :]
                here = sub == (0 if side == 0 else 7)
                moved = pltpu.roll(fld[t, rows(place(x_, source)), :], turn, 0)
                fld[t, rows(place(x_, r)), :] = jnp.where(here, halo, moved)
                moved = pltpu.roll(swapped[rows(place(x_, source)), :], turn, 0)
                swapped[rows(place(x_, r)), :] = jnp.where(here, pltpu.roll(halo, 64, 1), moved)
            return carry

        lax.fori_loop(0, CX, edge, 0, unroll=2)
        for side in range(2):
            arrive(hxr.at[t, side], hxss.at[t, side], hxrs.at[t, side], hx[side])
        open_x = [gx > 0, gx < 31]
        for side in range(2):
            for k in range(4):
                layer = k - 4 if side == 0 else 16 + k
                outer = k == 3 if side == 0 else k == 0
                for p in range(3):
                    pair = hxr[t, side, k, p].astype(F32)
                    if outer:
                        pair = pair + hxr[t, side, 4, p].astype(F32)
                    fld[t, rows(place(layer, 2 * p), 16), :] = jnp.where(open_x[side], pair, 0.0)

        def line(x_, carry):
            v = {r: fld[t, rows(place(x_, r)), :] for r in range(-2, 8)}
            w = {r: swapped[rows(place(x_, r)), :] for r in range(-2, 8)}
            for r in range(6):
                along = {
                    1: jnp.where(low_half, w[r - 1], w[r + 1]),
                    2: v[r - 1] + v[r + 1],
                    3: jnp.where(low_half, w[r + 1], w[r + 2]) + jnp.where(low_half, w[r - 2], w[r - 1]),
                    4: v[r - 2] + v[r + 2],
                }
                total = deep_z[rows((x_ * 6 + r) * 8), :] + (3.0 * STENCIL[0]) * v[r]
                for k in range(1, 5):
                    near = fld[t, rows(place(x_ - k, r)), :] + fld[t, rows(place(x_ + k, r)), :]
                    total = total + STENCIL[k] * (near + along[k])
                if t == 0:
                    before = prev_v[strided(x_, r), :]
                else:
                    before = fld[t - 1, rows(place(x_, r)), :]
                following = 2.0 * v[r] - before + speed[rows((x_ * 6 + r) * 8), :] * total
                if t < STEPS - 1:
                    fld[t + 1, rows(place(x_, r)), :] = following
                else:
                    last[rows((x_ * 6 + r) * 8), :] = following
            return carry

        lax.fori_loop(0, CX, line, 0)
        if t < STEPS - 1:
            send_halo(t + 1)
            inner(t + 1)

    lane8 = lax.broadcasted_iota(jnp.int32, (8, 128), 1)

    def multiply(s):
        blocks = kb[s].reshape(128, 1152)
        top = dot(f1a_s[...], blocks[:, :768])
        low = dot(f1b_s[...], blocks[:, 768:])
        value = top + jnp.concatenate([low[:32], low[32:]], axis=1)
        mine[s] = value[:16]
        theirs[s] = value[16:]
        send(theirs.at[s], got_s.at[s], cs.at[s], cr.at[s], cpeer)

    def partial(s):
        arrive(got_s.at[s], cs.at[s], cr.at[s], cpeer)
        value = mine[s] + got_s[s]
        largest = jnp.max(jnp.abs(value), axis=(0, 1), keepdims=True)
        largest = jnp.maximum(largest * 1.01, 1e-30).astype(BF16).astype(F32)
        code = encode(value, LIFT / largest)
        for q in range(6):
            v_s[16 * q : 16 * q + 16] = code[:, 128 * q : 128 * q + 128]
        v_s[96:128] = jnp.zeros((32, 128), F32)
        lines = [v_s[pl.ds(i, 8, stride=16), :] for i in range(16)]
        for m in range(4):
            for j in range(4):
                chunk = None
                for t in range(4):
                    piece = lines[(t % 2) * 8 + 2 * j + t // 2]
                    shift = (32 * (t - m)) % 128
                    piece = pltpu.roll(piece, shift, 1) if shift else piece
                    chunk = piece if t == 0 else jnp.where(lane8 < 32 * t, chunk, piece)
                w_s[6 * m : 6 * m + 6, 128 * j : 128 * j + 128] = chunk[0:6]
        fold = jnp.concatenate([w_s[16:24, 0:256], w_s[16:24, 256:512]], axis=0)
        mark = jnp.broadcast_to(largest, (16, 128))
        gb[s, x, zl] = jnp.concatenate([w_s[0:16, :], fold, mark], axis=1).astype(BF16)
        own = gb.at[s, x, zl]
        for d in range(3):
            send(own, own, gzs.at[s, d], gzr.at[s, d], lpeer[d])
        for d in (0, 2, 1):
            send(own, own, gxs.at[s, d, 3], gxr.at[s, d, zl], xpeer[d])

    def decode_row(s, row):
        def block(b, carry):
            got = gb[s, row, b].astype(F32)
            scale = got[:, 768:896] * (1.0 / LIFT)
            value = jnp.concatenate([decode(got[:, 128 * q : 128 * q + 128], scale) for q in range(6)], axis=1)
            start = (row * 4 + b) * 24
            g_s[s, rows(start, 16), :] = value[:, :512]
            g_s[s, rows(start + 16), :] = jnp.concatenate([value[0:8, 512:768], value[8:16, 512:768]], axis=1)
            return carry

        lax.fori_loop(0, 4, block, 0)

    def start_x(s):
        for d in (0, 2, 1):
            block = gb.at[s, x, (zl + 3 - d) % 4]
            arrive(block, gzs.at[s, d], gzr.at[s, d], lpeer[d])
            for e in (0, 2, 1):
                send(block, block, gxs.at[s, e, d], gxr.at[s, e, (zl + 3 - d) % 4], xpeer[e])
        decode_row(s, x)

    def end_x(s, d):
        source = (x + 3 - d) % 4
        for i in range(4):
            arrive(gb.at[s, source, i], gxs.at[s, d, i], gxr.at[s, d, i], xpeer[d])
        decode_row(s, source)

    def finish(s):
        high, low = halves(g_s[s])
        mixed = dot(f2p_s[...], high) + dot(f2p_s[...], low)
        high, low = halves(mixed)
        for j in range(4):
            cols = slice(128 * j, 128 * j + 128)
            deep = dot(jnp.concatenate([high[:, cols], low[:, cols]], axis=1), bd_s[...])
            for i in range(4):
                start = (i // 2) * 8 * YL + (2 * j + i % 2) * YL
                t_s[start : start + YL] = deep[:, 128 * i : 128 * i + 128]

        def line(j, carry):
            for r in range(6):
                even, odd, even_turned, odd_turned = (
                    t_s[pl.ds(j * YL + 2 * r + offset, 8, stride=12), :] for offset in (0, 1, 8 * YL, 8 * YL + 1)
                )
                for x2, term in (
                    (0, jnp.where(low_half, even, odd_turned)),
                    (1, jnp.where(low_half, even_turned, odd)),
                ):
                    x_ = x2 * 8 + j
                    here = rows((x_ * 6 + r) * 8)
                    if s < STEPS - 1:
                        term = term * fld[s + 1, rows(place(x_, r)), :]
                    else:
                        term = term * last[here, :]
                    if s > 0:
                        term = term + image[here, :]
                    if s < STEPS - 1:
                        image[here, :] = term
                    else:
                        out[strided(x_, r), :] = term
            return carry

        lax.fori_loop(0, 8, line, 0)

    def prepare():
        for load in loads[4:11]:
            load.wait()
        send(f1_v, f1_r, cs.at[STEPS], cr.at[STEPS], cpeer)
        f2p_s[...] = dot(f2_v[...], pf2_v[...]).astype(BF16)
        tall = dot(down_v[...], dep_v[...])
        wide = dot(tall.astype(BF16), across_v[...])
        block_row = lax.broadcasted_iota(jnp.int32, (128, 256), 0) // 32
        block_col = lax.broadcasted_iota(jnp.int32, (128, 256), 1) // 64
        swap_col = block_col + 1 - 2 * (block_col % 2)
        for i, col in enumerate((block_col, swap_col)):
            part = jnp.where(block_row == col, wide, 0.0).astype(BF16)
            bd_s[0:128, 256 * i : 256 * i + 256] = part
            bd_s[128:256, 256 * i : 256 * i + 256] = part

    def prepare_first():
        arrive(f1_r, cs.at[STEPS], cr.at[STEPS], cpeer)
        both = jnp.concatenate([f1_v[...], f1_r[...]], axis=0)
        both = dot(both, pf1_v[c]).astype(BF16)
        f1a_s[...] = both[:, :128]
        f1b_s[0:32] = both[:, 128:256]
        f1b_s[32:64] = both[:, 256:384]

    def first_fields():
        loads[1].wait()

        def spread(xs, carry):
            for xt in range(2):
                for r in range(6):
                    fld[0, rows(place(xt * 8 + xs, r)), :] = pres_v[pl.ds(xt * 384 + r * 8 + xs, 8, stride=48), :]
            return carry

        lax.fori_loop(0, 8, spread, 0)

    def speeds():
        loads[3].wait()
        last[...] = vel_v[...].astype(F32)

        def spread(xs, carry):
            for xt in range(2):
                for r in range(6):
                    speed[rows(((xt * 8 + xs) * 6 + r) * 8), :] = last[pl.ds(xt * 384 + r * 8 + xs, 8, stride=48), :]
            return carry

        lax.fori_loop(0, 8, spread, 0)
        loads[2].wait()

    pl.semaphore_wait(barrier, len(everyone))
    along_z(0, 0)
    along_z(0, 1)
    along_z(0, 2)
    first_fields()
    prepare()
    flush(3)
    along_z(1, 0)
    along_z(1, 1)
    along_z(1, 2)
    send_halo(0)
    loads[11].wait()
    inner(0)
    flush(3)
    along_z(2, 0)
    along_z(2, 1)
    along_z(2, 2)
    speeds()
    prepare_first()
    start_y(0)
    start_y(1)
    end_y(0)
    multiply(0)
    step(0)
    start_y(2)
    partial(0)
    end_y(1)
    multiply(1)
    partial(1)
    end_y(2)
    multiply(2)
    start_x(0)
    step(1)
    partial(2)
    start_x(1)
    end_x(0, 0)
    end_x(0, 2)
    start_x(2)
    end_x(1, 0)
    end_x(1, 2)
    end_x(0, 1)
    finish(0)
    step(2)
    end_x(2, 0)
    end_x(2, 2)
    end_x(1, 1)
    finish(1)
    end_x(2, 1)
    finish(2)
    flush()


def tiles(a):
    return a.reshape(2, 8, TILES, 128).transpose(0, 2, 1, 3).reshape(CX * TILES, 128)


def body(pressure, previous, velocity, tucker_core, first_factor, second_factor, depth_factor):
    args = (tiles(pressure), tiles(previous), tiles(velocity), tucker_core, first_factor, second_factor, depth_factor.T)
    args = args + constants()
    dma = pltpu.SemaphoreType.DMA
    image = pl.pallas_call(
        kernel,
        out_shape=pltpu.VMEM((CX * TILES, 128), F32),
        in_specs=[pl.BlockSpec(memory_space=pl.ANY)] * len(args),
        out_specs=pl.BlockSpec(memory_space=pltpu.VMEM),
        scratch_shapes=[
            pltpu.VMEM(a.shape, a.dtype) for a in args
        ]
        + [
            pltpu.VMEM((STEPS, 4, 4, 8, 1152), BF16),
            pltpu.VMEM((STEPS, 4, 4, 16, 896), BF16),
            pltpu.VMEM((STEPS, 24 * 10 * 8, 128), F32),
            pltpu.VMEM((24 * 10 * 8, 128), F32),
            pltpu.VMEM((CX * TILES, 128), F32),
            pltpu.VMEM((CX * TILES, 128), F32),
            pltpu.VMEM((CX * TILES, 128), F32),
            pltpu.VMEM((CX * TILES, 128), F32),
            pltpu.VMEM((STEPS, 2, 5, 3, 16, 128), BF16),
            pltpu.VMEM((STEPS, 2, 5, 3, 16, 128), BF16),
            pltpu.VMEM((STEPS, 2, 2, CX, 128), F32),
            pltpu.VMEM((STEPS, 2, 2, CX, 128), F32),
            pltpu.VMEM((128, 128), F32),
            pltpu.VMEM((24, 512), F32),
            pltpu.VMEM((STEPS, 384, 512), F32),
            pltpu.VMEM((2 * 8 * YL, 128), F32),
            pltpu.VMEM((256, 512), BF16),
            pltpu.VMEM((32, 128), BF16),
            pltpu.VMEM((64, 128), BF16),
            pltpu.VMEM((YL, 384), BF16),
            pltpu.VMEM((CX, 384), BF16),
            pltpu.VMEM((STEPS, CX, 768), F32),
            pltpu.VMEM((STEPS, CX, 768), F32),
            pltpu.VMEM((STEPS, CX, 768), F32),
            dma((len(args),)),
            dma((STEPS, 3)), dma((STEPS, 4)),
            dma((STEPS, 4)), dma((STEPS, 4)),
            dma((STEPS + 1,)), dma((STEPS + 1,)),
            dma((STEPS, 3)), dma((STEPS, 3)),
            dma((STEPS, 3, 4)), dma((STEPS, 3, 4)),
            dma((STEPS, 2)), dma((STEPS, 2)),
            dma((STEPS, 2)), dma((STEPS, 2)),
        ],
        compiler_params=pltpu.CompilerParams(
            collective_id=0, has_side_effects=True, vmem_limit_bytes=60 << 20
        ),
        name="image_steps",
    )(*args)
    return image.reshape(2, TILES, 8, 128).transpose(0, 2, 1, 3).reshape(CX, 8 * TILES * 16)


def solution(mesh):
    placed = (
        P("gx", "gy"),
        P("gx", "gy"),
        P("gx", "gy"),
        P(None, "gx", "gy"),
        P("gx", None),
        P("gy", None),
        P(),
    )
    return jax.shard_map(body, mesh=mesh, in_specs=placed, out_specs=P("gx", "gy"), check_vma=False)
```

```python
import functools

import jax
import jax.numpy as jnp
import numpy as np
from jax import lax
from jax.experimental import pallas as pl
from jax.experimental.pallas import tpu as pltpu
from jax.sharding import PartitionSpec as P

STENCIL = (-205.0 / 72.0, 8.0 / 5.0, -1.0 / 5.0, 8.0 / 315.0, -1.0 / 560.0)
MESH = pl.DeviceIdType.MESH
F32, BF16 = jnp.float32, jnp.bfloat16

STEPS = 3
CX = 16
NZ = 64
YL = 96
TILES = YL * NZ // 128
POWER = 13.0
LIFT = 512.0


def constants():
    first = np.zeros((2, 384, 384), np.float32)
    for core in range(2):
        for slot in range(16):
            block = slot * 2 + core
            for r in range(8):
                first[core, block * 12 + r, slot * 8 + r] = 1.0
            for r in range(4):
                first[core, block * 12 + 8 + r, 128 + slot * 8 + r] = 1.0
                first[core, block * 12 + 8 + r, 256 + slot * 8 + 4 + r] = 1.0
    second = np.zeros((384, 384), np.float32)
    for block in range(16):
        for m in range(4):
            for q in range(6):
                second[block * 24 + 4 * q + m, block * 24 + 6 * m + q] = 1.0
    down = np.tile(np.eye(32, dtype=np.float32), (4, 1))
    across = np.tile(np.eye(64, dtype=np.float32), (1, 4))
    z = np.arange(128)
    lines = np.zeros((128, 128), np.float64)
    for k in range(1, 5):
        near = np.abs(z[:, None] - z[None, :]) == k
        lines += STENCIL[k] * (near & (z[:, None] // 64 == z[None, :] // 64))
    swap = (np.abs(z[:, None] - z[None, :]) == 64).astype(np.float64)
    lines += STENCIL[1] * swap
    high = lines.astype(BF16)
    low = (lines - high.astype(np.float64)).astype(BF16)
    top = np.concatenate([high, swap.astype(BF16)], axis=1)
    near_z = np.concatenate([top, top, np.concatenate([low, np.zeros((128, 128), BF16)], axis=1)], axis=0)
    return tuple(jnp.asarray(a, BF16) for a in (first, second, down, across, near_z))


def dot(a, b):
    return lax.dot_general(a, b, (((1,), (0,)), ((), ())), preferred_element_type=F32)


def halves(a):
    high = a.astype(BF16)
    return high, (a - high.astype(F32)).astype(BF16)


def encode(value, scale):
    u = value * scale
    u2 = u * u
    u4 = u2 * u2
    return u4 * u4 * u4 * u


def decode(code, scale):
    size = jnp.abs(code)
    root = jnp.exp2(jnp.log2(jnp.maximum(size, 1e-38)) * (1.0 / POWER)) * scale
    root = jnp.where(size < 1e-37, 0.0, root)
    return jnp.where(code < 0.0, -root, root)


def place(x, r):
    return ((x + 4) * 10 + r + 2) * 8


def kernel(
    pres, prev, vel, core, f1, f2, dep, pf1, pf2, down, across, near_z,
    out,
    pres_v, prev_v, vel_v, core_v, f1_v, f2_v, dep_v, pf1_v, pf2_v, down_v, across_v, near_z_v,
    kb, gb, fld, swapped, deep_z, speed, last, image, hxs, hxr, hys, hyr, v_s, w_s, g_s, mixed_s, t_s, bd_s, f1a_s, f1b_s, f2p_s, f1_r, mine, theirs, got_s,
    lsem, zs, zr, ys, yr, cs, cr, gzs, gzr, gxs, gxr, hxss, hxrs, hyss, hyrs,
):
    gx, gy = lax.axis_index("gx"), lax.axis_index("gy")
    y, zh, c = gx // 8, (gx // 2) % 4, gx % 2
    x, zl = gy // 4, gy % 4

    def at(y_, zh_, c_):
        return ((y_ % 4) * 8 + (zh_ % 4) * 2 + c_, gy)

    def other(x_, zl_):
        return (gx, (x_ % 4) * 4 + zl_ % 4)

    zpeer = [at(y, zh + d, c) for d in (1, 2, 3)]
    ypeer = [at(y + d, zh, c) for d in (1, 2, 3)]
    cpeer = at(y, zh, 1 - c)
    lpeer = [other(x, zl + d) for d in (1, 2, 3)]
    xpeer = [other(x + d, zl) for d in (1, 2, 3)]
    hx = [((gx + 31) % 32, gy), ((gx + 1) % 32, gy)]
    hy = [(gx, (gy + 15) % 16), (gx, (gy + 1) % 16)]

    loads = [
        pltpu.make_async_copy(a, b, lsem.at[i])
        for i, (a, b) in enumerate(
            [
                (core, core_v), (pres, pres_v), (prev, prev_v), (vel, vel_v), (f1, f1_v), (pf1, pf1_v),
                (f2, f2_v), (pf2, pf2_v), (dep, dep_v), (down, down_v), (across, across_v), (near_z, near_z_v),
            ]
        )
    ]
    loads[0].start()
    barrier = pltpu.get_barrier_semaphore()
    everyone = zpeer + ypeer + [cpeer] + lpeer + xpeer + hx + hy
    for peer in everyone:
        pl.semaphore_signal(barrier, inc=1, device_id=peer, device_id_type=MESH)
    for load in loads[1:]:
        load.start()

    def remote(src, dst, ssem, rsem, peer):
        return pltpu.make_async_remote_copy(
            src_ref=src, dst_ref=dst, send_sem=ssem, recv_sem=rsem, device_id=peer, device_id_type=MESH
        )

    sent = []

    def send(src, dst, ssem, rsem, peer):
        copy = remote(src, dst, ssem, rsem, peer)
        copy.start()
        sent.append(copy)

    def arrive(dst, ssem, rsem, peer):
        remote(dst, dst, ssem, rsem, peer).wait_recv()

    def flush(count=None):
        for _ in range(len(sent) if count is None else count):
            sent.pop(0).wait_send()

    loads[0].wait()
    for s in range(STEPS):
        raw = core_v[s].astype(F32)
        tail = jnp.concatenate([raw[8:12, :384], raw[8:12, 384:]], axis=0)
        kb[s, y, zh] = jnp.concatenate([raw[:8], tail], axis=1).astype(BF16)
    def along_z(s, k):
        own = kb.at[s, y, zh]
        to = k + jnp.where(k >= zh, 1, 0)
        send(own, own, zs.at[s, k], zr.at[s, zh], at(y, to, c))

    def start_y(s):
        for d in range(3):
            source = (zh + 3 - d) % 4
            arrive(kb.at[s, y, source], zs.at[s, d], zr.at[s, source], zpeer[d])
        row = kb.at[s, y]
        for d in (0, 2, 1):
            send(row, row, ys.at[s, d], yr.at[s, d], ypeer[d])

    def end_y(s):
        for d in range(3):
            arrive(kb.at[s, (y + 3 - d) % 4], ys.at[s, d], yr.at[s, d], ypeer[d])


    low_half = lax.broadcasted_iota(jnp.int32, (8, 128), 1) < 64
    sub = lax.broadcasted_iota(jnp.int32, (8, 128), 0)

    def rows(start, count=8):
        return pl.ds(pl.multiple_of(start, 8), count)

    def strided(x_, r):
        return pl.ds((x_ // 8) * 384 + r * 8 + x_ % 8, 8, stride=48)

    def send_halo(t):
        for side in range(2):
            for k in range(4):
                layer = k if side == 0 else 12 + k
                outer = k == 0 if side == 0 else k == 3
                for p in range(3):
                    pair = fld[t, rows(place(layer, 2 * p), 16), :]
                    high = pair.astype(BF16)
                    hxs[t, side, k, p] = high
                    if outer:
                        hxs[t, side, 4, p] = (pair - high.astype(F32)).astype(BF16)
        for side in range(2):
            for i in range(2):
                for half in range(2):
                    start = place(8 * half, i) if side == 0 else place(8 * half, 4 + i) + 7
                    hys[t, side, i, 8 * half : 8 * half + 8] = fld[t, pl.ds(start, 8, stride=80), :]
        for side in (1, 0):
            send(hxs.at[t, side], hxr.at[t, 1 - side], hxss.at[t, side], hxrs.at[t, 1 - side], hx[side])
            send(hys.at[t, side], hyr.at[t, 1 - side], hyss.at[t, side], hyrs.at[t, 1 - side], hy[side])

    def inner(t):
        def run(q, carry):
            cells = jnp.concatenate([fld[t, rows(place(4 * q + k, 0), 48), :] for k in range(4)], axis=0)
            high, low = halves(cells)
            both = dot(jnp.concatenate([high, low], axis=1), near_z_v[0:256])
            along = both[:, :128] + dot(high, near_z_v[256:384, :128])
            for k in range(4):
                deep_z[rows((4 * q + k) * 48, 48), :] = along[48 * k : 48 * k + 48]
                swapped[rows(place(4 * q + k, 0), 48), :] = both[48 * k : 48 * k + 48, 128:]
            return carry

        lax.fori_loop(0, 4, run, 0)

    def step(t):
        for side in range(2):
            arrive(hyr.at[t, side], hyss.at[t, side], hyrs.at[t, side], hy[side])
        open_y = [gy > 0, gy < 15]
        edges = ((-2, 4, 0, 0, 1), (-1, 5, 0, 1, 1), (6, 0, 1, 0, 7), (7, 1, 1, 1, 7))
        for _, _, side, i, _ in edges:
            hyr[t, side, i] = jnp.where(open_y[side], hyr[t, side, i], 0.0)

        def edge(x_, carry):
            for r, source, side, i, turn in edges:
                halo = hyr[t, side, i, pl.ds(x_, 1), :]
                here = sub == (0 if side == 0 else 7)
                moved = pltpu.roll(fld[t, rows(place(x_, source)), :], turn, 0)
                fld[t, rows(place(x_, r)), :] = jnp.where(here, halo, moved)
                moved = pltpu.roll(swapped[rows(place(x_, source)), :], turn, 0)
                swapped[rows(place(x_, r)), :] = jnp.where(here, pltpu.roll(halo, 64, 1), moved)
            return carry

        lax.fori_loop(0, CX, edge, 0, unroll=2)
        for side in range(2):
            arrive(hxr.at[t, side], hxss.at[t, side], hxrs.at[t, side], hx[side])
        open_x = [gx > 0, gx < 31]
        for side in range(2):
            for k in range(4):
                layer = k - 4 if side == 0 else 16 + k
                outer = k == 3 if side == 0 else k == 0
                for p in range(3):
                    pair = hxr[t, side, k, p].astype(F32)
                    if outer:
                        pair = pair + hxr[t, side, 4, p].astype(F32)
                    fld[t, rows(place(layer, 2 * p), 16), :] = jnp.where(open_x[side], pair, 0.0)

        def line(x_, carry):
            v = {r: fld[t, rows(place(x_, r)), :] for r in range(-2, 8)}
            w = {r: swapped[rows(place(x_, r)), :] for r in range(-2, 8)}
            for r in range(6):
                along = {
                    1: jnp.where(low_half, w[r - 1], w[r + 1]),
                    2: v[r - 1] + v[r + 1],
                    3: jnp.where(low_half, w[r + 1], w[r + 2]) + jnp.where(low_half, w[r - 2], w[r - 1]),
                    4: v[r - 2] + v[r + 2],
                }
                total = deep_z[rows((x_ * 6 + r) * 8), :] + (3.0 * STENCIL[0]) * v[r]
                for k in range(1, 5):
                    near = fld[t, rows(place(x_ - k, r)), :] + fld[t, rows(place(x_ + k, r)), :]
                    total = total + STENCIL[k] * (near + along[k])
                if t == 0:
                    before = prev_v[strided(x_, r), :]
                else:
                    before = fld[t - 1, rows(place(x_, r)), :]
                following = 2.0 * v[r] - before + speed[rows((x_ * 6 + r) * 8), :] * total
                if t < STEPS - 1:
                    fld[t + 1, rows(place(x_, r)), :] = following
                else:
                    last[rows((x_ * 6 + r) * 8), :] = following
            return carry

        lax.fori_loop(0, CX, line, 0)
        if t < STEPS - 1:
            send_halo(t + 1)
            inner(t + 1)

    lane8 = lax.broadcasted_iota(jnp.int32, (8, 128), 1)

    def multiply(s):
        blocks = kb[s].reshape(128, 1152)
        top = dot(f1a_s[...], blocks[:, :768])
        low = dot(f1b_s[...], blocks[:, 768:])
        value = top + jnp.concatenate([low[:32], low[32:]], axis=1)
        mine[s] = value[:16]
        theirs[s] = value[16:]
        send(theirs.at[s], got_s.at[s], cs.at[s], cr.at[s], cpeer)

    def partial(s):
        arrive(got_s.at[s], cs.at[s], cr.at[s], cpeer)
        value = mine[s] + got_s[s]
        largest = jnp.max(jnp.abs(value), axis=(0, 1), keepdims=True)
        largest = jnp.maximum(largest * 1.01, 1e-30).astype(BF16).astype(F32)
        code = encode(value, LIFT / largest)
        for q in range(6):
            v_s[16 * q : 16 * q + 16] = code[:, 128 * q : 128 * q + 128]
        v_s[96:128] = jnp.zeros((32, 128), F32)
        lines = [v_s[pl.ds(i, 8, stride=16), :] for i in range(16)]
        for m in range(4):
            for j in range(4):
                chunk = None
                for t in range(4):
                    piece = lines[(t % 2) * 8 + 2 * j + t // 2]
                    shift = (32 * (t - m)) % 128
                    piece = pltpu.roll(piece, shift, 1) if shift else piece
                    chunk = piece if t == 0 else jnp.where(lane8 < 32 * t, chunk, piece)
                w_s[6 * m : 6 * m + 6, 128 * j : 128 * j + 128] = chunk[0:6]
        mark = jnp.broadcast_to(largest, (8, 128))
        gb[s, x, zl] = jnp.concatenate([w_s[0:8, :], w_s[8:16, :], w_s[16:24, :], mark], axis=1).astype(BF16)
        own = gb.at[s, x, zl]
        for d in range(3):
            send(own, own, gzs.at[s, d], gzr.at[s, d], lpeer[d])
        for d in (0, 2, 1):
            send(own, own, gxs.at[s, d, 3], gxr.at[s, d, zl], xpeer[d])

    def decode_row(s, row, fresh=False):
        def block(b, carry):
            got = gb[s, row, b].astype(F32)
            scale = got[:, 1536:1664] * (1.0 / LIFT)
            for q in range(12):
                value = decode(got[:, 128 * q : 128 * q + 128], scale)
                g_s[rows(b * 24 + q // 4 * 8), 128 * (q % 4) : 128 * (q % 4) + 128] = value
            return carry

        lax.fori_loop(0, 4, block, 0)
        high, low = halves(g_s[...])
        part = dot(f2p_s[row], jnp.concatenate([high, low], axis=0))
        mixed_s[s] = part if fresh else mixed_s[s] + part

    def start_x(s):
        for d in (0, 2, 1):
            block = gb.at[s, x, (zl + 3 - d) % 4]
            arrive(block, gzs.at[s, d], gzr.at[s, d], lpeer[d])
            for e in (0, 2, 1):
                send(block, block, gxs.at[s, e, d], gxr.at[s, e, (zl + 3 - d) % 4], xpeer[e])
        decode_row(s, x, True)

    def end_x(s, d):
        source = (x + 3 - d) % 4
        for i in range(4):
            arrive(gb.at[s, source, i], gxs.at[s, d, i], gxr.at[s, d, i], xpeer[d])
        decode_row(s, source)

    def finish(s):
        high, low = halves(mixed_s[s])
        for j in range(4):
            cols = slice(128 * j, 128 * j + 128)
            deep = dot(jnp.concatenate([high[:, cols], low[:, cols]], axis=1), bd_s[...])
            for i in range(4):
                start = (i // 2) * 8 * YL + (2 * j + i % 2) * YL
                t_s[start : start + YL] = deep[:, 128 * i : 128 * i + 128]

        def line(j, carry):
            for r in range(6):
                even, odd, even_turned, odd_turned = (
                    t_s[pl.ds(j * YL + 2 * r + offset, 8, stride=12), :] for offset in (0, 1, 8 * YL, 8 * YL + 1)
                )
                for x2, term in (
                    (0, jnp.where(low_half, even, odd_turned)),
                    (1, jnp.where(low_half, even_turned, odd)),
                ):
                    x_ = x2 * 8 + j
                    here = rows((x_ * 6 + r) * 8)
                    if s < STEPS - 1:
                        term = term * fld[s + 1, rows(place(x_, r)), :]
                    else:
                        term = term * last[here, :]
                    if s > 0:
                        term = term + image[here, :]
                    if s < STEPS - 1:
                        image[here, :] = term
                    else:
                        out[strided(x_, r), :] = term
            return carry

        lax.fori_loop(0, 8, line, 0)

    def prepare():
        for load in loads[4:11]:
            load.wait()
        send(f1_v, f1_r, cs.at[STEPS], cr.at[STEPS], cpeer)
        f2p = dot(f2_v[...], pf2_v[...]).astype(BF16)
        for row in range(4):
            part = f2p[:, 96 * row : 96 * row + 96]
            f2p_s[row] = jnp.concatenate([part, part], axis=1)
        tall = dot(down_v[...], dep_v[...])
        wide = dot(tall.astype(BF16), across_v[...])
        block_row = lax.broadcasted_iota(jnp.int32, (128, 256), 0) // 32
        block_col = lax.broadcasted_iota(jnp.int32, (128, 256), 1) // 64
        swap_col = block_col + 1 - 2 * (block_col % 2)
        for i, col in enumerate((block_col, swap_col)):
            part = jnp.where(block_row == col, wide, 0.0).astype(BF16)
            bd_s[0:128, 256 * i : 256 * i + 256] = part
            bd_s[128:256, 256 * i : 256 * i + 256] = part

    def prepare_first():
        arrive(f1_r, cs.at[STEPS], cr.at[STEPS], cpeer)
        both = jnp.concatenate([f1_v[...], f1_r[...]], axis=0)
        both = dot(both, pf1_v[c]).astype(BF16)
        f1a_s[...] = both[:, :128]
        f1b_s[0:32] = both[:, 128:256]
        f1b_s[32:64] = both[:, 256:384]

    def first_fields():
        loads[1].wait()

        def spread(xs, carry):
            for xt in range(2):
                for r in range(6):
                    fld[0, rows(place(xt * 8 + xs, r)), :] = pres_v[pl.ds(xt * 384 + r * 8 + xs, 8, stride=48), :]
            return carry

        lax.fori_loop(0, 8, spread, 0)

    def speeds():
        loads[3].wait()
        last[...] = vel_v[...].astype(F32)

        def spread(xs, carry):
            for xt in range(2):
                for r in range(6):
                    speed[rows(((xt * 8 + xs) * 6 + r) * 8), :] = last[pl.ds(xt * 384 + r * 8 + xs, 8, stride=48), :]
            return carry

        lax.fori_loop(0, 8, spread, 0)
        loads[2].wait()

    pl.semaphore_wait(barrier, len(everyone))
    along_z(0, 0)
    along_z(0, 1)
    along_z(0, 2)
    first_fields()
    prepare()
    flush(3)
    along_z(1, 0)
    along_z(1, 1)
    along_z(1, 2)
    send_halo(0)
    loads[11].wait()
    inner(0)
    flush(3)
    along_z(2, 0)
    along_z(2, 1)
    along_z(2, 2)
    speeds()
    prepare_first()
    start_y(0)
    start_y(1)
    end_y(0)
    multiply(0)
    partial(0)
    start_y(2)
    step(0)
    end_y(1)
    multiply(1)
    partial(1)
    start_x(0)
    end_y(2)
    multiply(2)
    partial(2)
    start_x(1)
    step(1)
    start_x(2)
    end_x(0, 0)
    end_x(0, 2)
    end_x(0, 1)
    finish(0)
    end_x(1, 0)
    end_x(1, 2)
    step(2)
    end_x(1, 1)
    finish(1)
    end_x(2, 0)
    end_x(2, 2)
    end_x(2, 1)
    finish(2)
    flush()


def tiles(a):
    return a.reshape(2, 8, TILES, 128).transpose(0, 2, 1, 3).reshape(CX * TILES, 128)


def body(pressure, previous, velocity, tucker_core, first_factor, second_factor, depth_factor):
    args = (tiles(pressure), tiles(previous), tiles(velocity), tucker_core, first_factor, second_factor, depth_factor.T)
    args = args + constants()
    dma = pltpu.SemaphoreType.DMA
    image = pl.pallas_call(
        kernel,
        out_shape=pltpu.VMEM((CX * TILES, 128), F32),
        in_specs=[pl.BlockSpec(memory_space=pl.ANY)] * len(args),
        out_specs=pl.BlockSpec(memory_space=pltpu.VMEM),
        scratch_shapes=[
            pltpu.VMEM(a.shape, a.dtype) for a in args
        ]
        + [
            pltpu.VMEM((STEPS, 4, 4, 8, 1152), BF16),
            pltpu.VMEM((STEPS, 4, 4, 8, 1664), BF16),
            pltpu.VMEM((STEPS, 24 * 10 * 8, 128), F32),
            pltpu.VMEM((24 * 10 * 8, 128), F32),
            pltpu.VMEM((CX * TILES, 128), F32),
            pltpu.VMEM((CX * TILES, 128), F32),
            pltpu.VMEM((CX * TILES, 128), F32),
            pltpu.VMEM((CX * TILES, 128), F32),
            pltpu.VMEM((STEPS, 2, 5, 3, 16, 128), BF16),
            pltpu.VMEM((STEPS, 2, 5, 3, 16, 128), BF16),
            pltpu.VMEM((STEPS, 2, 2, CX, 128), F32),
            pltpu.VMEM((STEPS, 2, 2, CX, 128), F32),
            pltpu.VMEM((128, 128), F32),
            pltpu.VMEM((24, 512), F32),
            pltpu.VMEM((96, 512), F32),
            pltpu.VMEM((STEPS, YL, 512), F32),
            pltpu.VMEM((2 * 8 * YL, 128), F32),
            pltpu.VMEM((256, 512), BF16),
            pltpu.VMEM((32, 128), BF16),
            pltpu.VMEM((64, 128), BF16),
            pltpu.VMEM((4, YL, 192), BF16),
            pltpu.VMEM((CX, 384), BF16),
            pltpu.VMEM((STEPS, CX, 768), F32),
            pltpu.VMEM((STEPS, CX, 768), F32),
            pltpu.VMEM((STEPS, CX, 768), F32),
            dma((len(args),)),
            dma((STEPS, 3)), dma((STEPS, 4)),
            dma((STEPS, 4)), dma((STEPS, 4)),
            dma((STEPS + 1,)), dma((STEPS + 1,)),
            dma((STEPS, 3)), dma((STEPS, 3)),
            dma((STEPS, 3, 4)), dma((STEPS, 3, 4)),
            dma((STEPS, 2)), dma((STEPS, 2)),
            dma((STEPS, 2)), dma((STEPS, 2)),
        ],
        compiler_params=pltpu.CompilerParams(
            collective_id=0, has_side_effects=True, vmem_limit_bytes=60 << 20
        ),
        name="image_steps",
    )(*args)
    return image.reshape(2, TILES, 8, 128).transpose(0, 2, 1, 3).reshape(CX, 8 * TILES * 16)


def solution(mesh):
    placed = (
        P("gx", "gy"),
        P("gx", "gy"),
        P("gx", "gy"),
        P(None, "gx", "gy"),
        P("gx", None),
        P("gy", None),
        P(),
    )
    return jax.shard_map(body, mesh=mesh, in_specs=placed, out_specs=P("gx", "gy"), check_vma=False)
```

```python
import functools

import jax
import jax.numpy as jnp
import numpy as np
from jax import lax
from jax.experimental import pallas as pl
from jax.experimental.pallas import tpu as pltpu
from jax.sharding import PartitionSpec as P

STENCIL = (-205.0 / 72.0, 8.0 / 5.0, -1.0 / 5.0, 8.0 / 315.0, -1.0 / 560.0)
MESH = pl.DeviceIdType.MESH
F32, BF16 = jnp.float32, jnp.bfloat16

STEPS = 3
CX = 16
NZ = 64
YL = 96
TILES = YL * NZ // 128
POWER = 13.0
LIFT = 512.0


def constants():
    first = np.zeros((2, 384, 384), np.float32)
    for core in range(2):
        for slot in range(16):
            block = slot * 2 + core
            for r in range(8):
                first[core, block * 12 + r, slot * 8 + r] = 1.0
            for r in range(4):
                first[core, block * 12 + 8 + r, 128 + slot * 8 + r] = 1.0
                first[core, block * 12 + 8 + r, 256 + slot * 8 + 4 + r] = 1.0
    second = np.zeros((384, 384), np.float32)
    for block in range(16):
        for m in range(4):
            for q in range(6):
                second[block * 24 + 4 * q + m, block * 24 + 6 * m + q] = 1.0
    down = np.tile(np.eye(32, dtype=np.float32), (4, 1))
    across = np.tile(np.eye(64, dtype=np.float32), (1, 4))
    z = np.arange(128)
    lines = np.zeros((128, 128), np.float64)
    for k in range(1, 5):
        near = np.abs(z[:, None] - z[None, :]) == k
        lines += STENCIL[k] * (near & (z[:, None] // 64 == z[None, :] // 64))
    swap = (np.abs(z[:, None] - z[None, :]) == 64).astype(np.float64)
    lines += STENCIL[1] * swap
    high = lines.astype(BF16)
    low = (lines - high.astype(np.float64)).astype(BF16)
    top = np.concatenate([high, swap.astype(BF16)], axis=1)
    near_z = np.concatenate([top, top, np.concatenate([low, np.zeros((128, 128), BF16)], axis=1)], axis=0)
    return tuple(jnp.asarray(a, BF16) for a in (first, second, down, across, near_z))


def dot(a, b):
    return lax.dot_general(a, b, (((1,), (0,)), ((), ())), preferred_element_type=F32)


def halves(a):
    high = a.astype(BF16)
    return high, (a - high.astype(F32)).astype(BF16)


def encode(value, scale):
    u = value * scale
    u2 = u * u
    u4 = u2 * u2
    return u4 * u4 * u4 * u


def decode(code, scale):
    size = jnp.abs(code)
    root = jnp.exp2(jnp.log2(jnp.maximum(size, 1e-38)) * (1.0 / POWER)) * scale
    root = jnp.where(size < 1e-37, 0.0, root)
    return jnp.where(code < 0.0, -root, root)


def place(x, r):
    return ((x + 4) * 10 + r + 2) * 8


def kernel(
    pres, prev, vel, core, f1, f2, dep, pf1, pf2, down, across, near_z,
    out,
    pres_v, prev_v, vel_v, core_v, f1_v, f2_v, dep_v, pf1_v, pf2_v, down_v, across_v, near_z_v,
    kb, gb, fld, swapped, deep_z, speed, last, image, hxs, hxr, hys, hyr, v_s, w_s, g_s, mixed_s, t_s, bd_s, f1a_s, f1b_s, f2p_s, f1_r, mine, theirs, got_s,
    lsem, zs, zr, ys, yr, cs, cr, gzs, gzr, gxs, gxr, hxss, hxrs, hyss, hyrs,
):
    gx, gy = lax.axis_index("gx"), lax.axis_index("gy")
    y, zh, c = gx // 8, (gx // 2) % 4, gx % 2
    x, zl = gy // 4, gy % 4

    def at(y_, zh_, c_):
        return ((y_ % 4) * 8 + (zh_ % 4) * 2 + c_, gy)

    def other(x_, zl_):
        return (gx, (x_ % 4) * 4 + zl_ % 4)

    zpeer = [at(y, zh + d, c) for d in (1, 2, 3)]
    ypeer = [at(y + d, zh, c) for d in (1, 2, 3)]
    cpeer = at(y, zh, 1 - c)
    lpeer = [other(x, zl + d) for d in (1, 2, 3)]
    xpeer = [other(x + d, zl) for d in (1, 2, 3)]
    hx = [((gx + 31) % 32, gy), ((gx + 1) % 32, gy)]
    hy = [(gx, (gy + 15) % 16), (gx, (gy + 1) % 16)]

    loads = [
        pltpu.make_async_copy(a, b, lsem.at[i])
        for i, (a, b) in enumerate(
            [
                (core, core_v), (pres, pres_v), (prev, prev_v), (vel, vel_v), (f1, f1_v), (pf1, pf1_v),
                (f2, f2_v), (pf2, pf2_v), (dep, dep_v), (down, down_v), (across, across_v), (near_z, near_z_v),
            ]
        )
    ]
    loads[0].start()
    barrier = pltpu.get_barrier_semaphore()
    everyone = zpeer + ypeer + [cpeer] + lpeer + xpeer + hx + hy
    for peer in everyone:
        pl.semaphore_signal(barrier, inc=1, device_id=peer, device_id_type=MESH)
    for load in loads[1:]:
        load.start()

    def remote(src, dst, ssem, rsem, peer):
        return pltpu.make_async_remote_copy(
            src_ref=src, dst_ref=dst, send_sem=ssem, recv_sem=rsem, device_id=peer, device_id_type=MESH
        )

    sent = []

    def send(src, dst, ssem, rsem, peer):
        copy = remote(src, dst, ssem, rsem, peer)
        copy.start()
        sent.append(copy)

    def arrive(dst, ssem, rsem, peer):
        remote(dst, dst, ssem, rsem, peer).wait_recv()

    def flush(count=None):
        for _ in range(len(sent) if count is None else count):
            sent.pop(0).wait_send()

    loads[0].wait()
    for s in range(STEPS):
        raw = core_v[s].astype(F32)
        tail = jnp.concatenate([raw[8:12, :384], raw[8:12, 384:]], axis=0)
        kb[s, y, zh] = jnp.concatenate([raw[:8], tail], axis=1).astype(BF16)
    def along_z(s, k):
        own = kb.at[s, y, zh]
        to = k + jnp.where(k >= zh, 1, 0)
        send(own, own, zs.at[s, k], zr.at[s, zh], at(y, to, c))

    def start_y(s):
        for d in range(3):
            source = (zh + 3 - d) % 4
            arrive(kb.at[s, y, source], zs.at[s, d], zr.at[s, source], zpeer[d])
        row = kb.at[s, y]
        for d in (1, 0, 2):
            send(row, row, ys.at[s, d], yr.at[s, d], ypeer[d])

    def end_y(s):
        for d in range(3):
            arrive(kb.at[s, (y + 3 - d) % 4], ys.at[s, d], yr.at[s, d], ypeer[d])


    low_half = lax.broadcasted_iota(jnp.int32, (8, 128), 1) < 64
    sub = lax.broadcasted_iota(jnp.int32, (8, 128), 0)

    def rows(start, count=8):
        return pl.ds(pl.multiple_of(start, 8), count)

    def strided(x_, r):
        return pl.ds((x_ // 8) * 384 + r * 8 + x_ % 8, 8, stride=48)

    def send_halo(t):
        for side in range(2):
            for k in range(4):
                layer = k if side == 0 else 12 + k
                outer = k == 0 if side == 0 else k == 3
                for p in range(3):
                    pair = fld[t, rows(place(layer, 2 * p), 16), :]
                    high = pair.astype(BF16)
                    hxs[t, side, k, p] = high
                    if outer:
                        hxs[t, side, 4, p] = (pair - high.astype(F32)).astype(BF16)
        for side in range(2):
            for i in range(2):
                for half in range(2):
                    start = place(8 * half, i) if side == 0 else place(8 * half, 4 + i) + 7
                    hys[t, side, i, 8 * half : 8 * half + 8] = fld[t, pl.ds(start, 8, stride=80), :]
        for side in (1, 0):
            send(hxs.at[t, side], hxr.at[t, 1 - side], hxss.at[t, side], hxrs.at[t, 1 - side], hx[side])
            send(hys.at[t, side], hyr.at[t, 1 - side], hyss.at[t, side], hyrs.at[t, 1 - side], hy[side])

    def inner(t):
        def run(q, carry):
            cells = jnp.concatenate([fld[t, rows(place(4 * q + k, 0), 48), :] for k in range(4)], axis=0)
            high, low = halves(cells)
            both = dot(jnp.concatenate([high, low], axis=1), near_z_v[0:256])
            along = both[:, :128] + dot(high, near_z_v[256:384, :128])
            for k in range(4):
                deep_z[rows((4 * q + k) * 48, 48), :] = along[48 * k : 48 * k + 48]
                swapped[rows(place(4 * q + k, 0), 48), :] = both[48 * k : 48 * k + 48, 128:]
            return carry

        lax.fori_loop(0, 4, run, 0)

    def step(t):
        for side in range(2):
            arrive(hyr.at[t, side], hyss.at[t, side], hyrs.at[t, side], hy[side])
        open_y = [gy > 0, gy < 15]
        edges = ((-2, 4, 0, 0, 1), (-1, 5, 0, 1, 1), (6, 0, 1, 0, 7), (7, 1, 1, 1, 7))
        for _, _, side, i, _ in edges:
            hyr[t, side, i] = jnp.where(open_y[side], hyr[t, side, i], 0.0)

        def edge(x_, carry):
            for r, source, side, i, turn in edges:
                halo = hyr[t, side, i, pl.ds(x_, 1), :]
                here = sub == (0 if side == 0 else 7)
                moved = pltpu.roll(fld[t, rows(place(x_, source)), :], turn, 0)
                fld[t, rows(place(x_, r)), :] = jnp.where(here, halo, moved)
                moved = pltpu.roll(swapped[rows(place(x_, source)), :], turn, 0)
                swapped[rows(place(x_, r)), :] = jnp.where(here, pltpu.roll(halo, 64, 1), moved)
            return carry

        lax.fori_loop(0, CX, edge, 0, unroll=2)
        for side in range(2):
            arrive(hxr.at[t, side], hxss.at[t, side], hxrs.at[t, side], hx[side])
        open_x = [gx > 0, gx < 31]
        for side in range(2):
            for k in range(4):
                layer = k - 4 if side == 0 else 16 + k
                outer = k == 3 if side == 0 else k == 0
                for p in range(3):
                    pair = hxr[t, side, k, p].astype(F32)
                    if outer:
                        pair = pair + hxr[t, side, 4, p].astype(F32)
                    fld[t, rows(place(layer, 2 * p), 16), :] = jnp.where(open_x[side], pair, 0.0)

        def line(x_, carry):
            v = {r: fld[t, rows(place(x_, r)), :] for r in range(-2, 8)}
            w = {r: swapped[rows(place(x_, r)), :] for r in range(-2, 8)}
            for r in range(6):
                along = {
                    1: jnp.where(low_half, w[r - 1], w[r + 1]),
                    2: v[r - 1] + v[r + 1],
                    3: jnp.where(low_half, w[r + 1], w[r + 2]) + jnp.where(low_half, w[r - 2], w[r - 1]),
                    4: v[r - 2] + v[r + 2],
                }
                total = deep_z[rows((x_ * 6 + r) * 8), :] + (3.0 * STENCIL[0]) * v[r]
                for k in range(1, 5):
                    near = fld[t, rows(place(x_ - k, r)), :] + fld[t, rows(place(x_ + k, r)), :]
                    total = total + STENCIL[k] * (near + along[k])
                if t == 0:
                    before = prev_v[strided(x_, r), :]
                else:
                    before = fld[t - 1, rows(place(x_, r)), :]
                following = 2.0 * v[r] - before + speed[rows((x_ * 6 + r) * 8), :] * total
                if t < STEPS - 1:
                    fld[t + 1, rows(place(x_, r)), :] = following
                else:
                    last[rows((x_ * 6 + r) * 8), :] = following
            return carry

        lax.fori_loop(0, CX, line, 0)
        if t < STEPS - 1:
            send_halo(t + 1)
            inner(t + 1)

    lane8 = lax.broadcasted_iota(jnp.int32, (8, 128), 1)

    def multiply(s):
        blocks = kb[s].reshape(128, 1152)
        top = dot(f1a_s[...], blocks[:, :768])
        low = dot(f1b_s[...], blocks[:, 768:])
        value = top + jnp.concatenate([low[:32], low[32:]], axis=1)
        mine[s] = value[:16]
        theirs[s] = value[16:]
        send(theirs.at[s], got_s.at[s], cs.at[s], cr.at[s], cpeer)

    def partial(s):
        arrive(got_s.at[s], cs.at[s], cr.at[s], cpeer)
        value = mine[s] + got_s[s]
        largest = jnp.max(jnp.abs(value), axis=(0, 1), keepdims=True)
        largest = jnp.maximum(largest * 1.01, 1e-30).astype(BF16).astype(F32)
        code = encode(value, LIFT / largest)
        for q in range(6):
            v_s[16 * q : 16 * q + 16] = code[:, 128 * q : 128 * q + 128]
        v_s[96:128] = jnp.zeros((32, 128), F32)
        lines = [v_s[pl.ds(i, 8, stride=16), :] for i in range(16)]
        for m in range(4):
            for j in range(4):
                chunk = None
                for t in range(4):
                    piece = lines[(t % 2) * 8 + 2 * j + t // 2]
                    shift = (32 * (t - m)) % 128
                    piece = pltpu.roll(piece, shift, 1) if shift else piece
                    chunk = piece if t == 0 else jnp.where(lane8 < 32 * t, chunk, piece)
                w_s[6 * m : 6 * m + 6, 128 * j : 128 * j + 128] = chunk[0:6]
        mark = jnp.broadcast_to(largest, (8, 128))
        gb[s, x, zl] = jnp.concatenate([w_s[0:8, :], w_s[8:16, :], w_s[16:24, :], mark], axis=1).astype(BF16)
        own = gb.at[s, x, zl]
        for d in range(3):
            send(own, own, gzs.at[s, d], gzr.at[s, d], lpeer[d])
        for d in (1, 0, 2):
            send(own, own, gxs.at[s, d, 3], gxr.at[s, d, zl], xpeer[d])

    def decode_row(s, row, fresh=False):
        def block(b, carry):
            got = gb[s, row, b].astype(F32)
            scale = got[:, 1536:1664] * (1.0 / LIFT)
            for q in range(12):
                value = decode(got[:, 128 * q : 128 * q + 128], scale)
                g_s[rows(b * 24 + q // 4 * 8), 128 * (q % 4) : 128 * (q % 4) + 128] = value
            return carry

        lax.fori_loop(0, 4, block, 0)
        high, low = halves(g_s[...])
        part = dot(f2p_s[row], jnp.concatenate([high, low], axis=0))
        mixed_s[s] = part if fresh else mixed_s[s] + part

    def start_x(s):
        for d in (0, 2, 1):
            block = gb.at[s, x, (zl + 3 - d) % 4]
            arrive(block, gzs.at[s, d], gzr.at[s, d], lpeer[d])
            for e in (1, 0, 2):
                send(block, block, gxs.at[s, e, d], gxr.at[s, e, (zl + 3 - d) % 4], xpeer[e])
        decode_row(s, x, True)

    def end_x(s, d):
        source = (x + 3 - d) % 4
        for i in range(4):
            arrive(gb.at[s, source, i], gxs.at[s, d, i], gxr.at[s, d, i], xpeer[d])
        decode_row(s, source)

    def finish(s):
        high, low = halves(mixed_s[s])
        for j in range(4):
            cols = slice(128 * j, 128 * j + 128)
            deep = dot(jnp.concatenate([high[:, cols], low[:, cols]], axis=1), bd_s[...])
            for i in range(4):
                start = (i // 2) * 8 * YL + (2 * j + i % 2) * YL
                t_s[start : start + YL] = deep[:, 128 * i : 128 * i + 128]

        def line(j, carry):
            for r in range(6):
                even, odd, even_turned, odd_turned = (
                    t_s[pl.ds(j * YL + 2 * r + offset, 8, stride=12), :] for offset in (0, 1, 8 * YL, 8 * YL + 1)
                )
                for x2, term in (
                    (0, jnp.where(low_half, even, odd_turned)),
                    (1, jnp.where(low_half, even_turned, odd)),
                ):
                    x_ = x2 * 8 + j
                    here = rows((x_ * 6 + r) * 8)
                    if s < STEPS - 1:
                        term = term * fld[s + 1, rows(place(x_, r)), :]
                    else:
                        term = term * last[here, :]
                    if s > 0:
                        term = term + image[here, :]
                    if s < STEPS - 1:
                        image[here, :] = term
                    else:
                        out[strided(x_, r), :] = term
            return carry

        lax.fori_loop(0, 8, line, 0)

    def prepare():
        for load in loads[4:11]:
            load.wait()
        send(f1_v, f1_r, cs.at[STEPS], cr.at[STEPS], cpeer)
        f2p = dot(f2_v[...], pf2_v[...]).astype(BF16)
        for row in range(4):
            part = f2p[:, 96 * row : 96 * row + 96]
            f2p_s[row] = jnp.concatenate([part, part], axis=1)
        tall = dot(down_v[...], dep_v[...])
        wide = dot(tall.astype(BF16), across_v[...])
        block_row = lax.broadcasted_iota(jnp.int32, (128, 256), 0) // 32
        block_col = lax.broadcasted_iota(jnp.int32, (128, 256), 1) // 64
        swap_col = block_col + 1 - 2 * (block_col % 2)
        for i, col in enumerate((block_col, swap_col)):
            part = jnp.where(block_row == col, wide, 0.0).astype(BF16)
            bd_s[0:128, 256 * i : 256 * i + 256] = part
            bd_s[128:256, 256 * i : 256 * i + 256] = part

    def prepare_first():
        arrive(f1_r, cs.at[STEPS], cr.at[STEPS], cpeer)
        both = jnp.concatenate([f1_v[...], f1_r[...]], axis=0)
        both = dot(both, pf1_v[c]).astype(BF16)
        f1a_s[...] = both[:, :128]
        f1b_s[0:32] = both[:, 128:256]
        f1b_s[32:64] = both[:, 256:384]

    def first_fields():
        loads[1].wait()

        def spread(xs, carry):
            for xt in range(2):
                for r in range(6):
                    fld[0, rows(place(xt * 8 + xs, r)), :] = pres_v[pl.ds(xt * 384 + r * 8 + xs, 8, stride=48), :]
            return carry

        lax.fori_loop(0, 8, spread, 0)

    def speeds():
        loads[3].wait()
        last[...] = vel_v[...].astype(F32)

        def spread(xs, carry):
            for xt in range(2):
                for r in range(6):
                    speed[rows(((xt * 8 + xs) * 6 + r) * 8), :] = last[pl.ds(xt * 384 + r * 8 + xs, 8, stride=48), :]
            return carry

        lax.fori_loop(0, 8, spread, 0)
        loads[2].wait()

    pl.semaphore_wait(barrier, len(everyone))
    along_z(0, 0)
    along_z(0, 1)
    along_z(0, 2)
    first_fields()
    prepare()
    flush(3)
    along_z(1, 0)
    along_z(1, 1)
    along_z(1, 2)
    send_halo(0)
    loads[11].wait()
    inner(0)
    flush(3)
    along_z(2, 0)
    along_z(2, 1)
    along_z(2, 2)
    speeds()
    prepare_first()
    start_y(0)
    start_y(1)
    end_y(0)
    multiply(0)
    partial(0)
    start_y(2)
    step(0)
    end_y(1)
    multiply(1)
    partial(1)
    start_x(0)
    end_y(2)
    multiply(2)
    partial(2)
    start_x(1)
    step(1)
    start_x(2)
    end_x(0, 0)
    end_x(0, 2)
    end_x(0, 1)
    finish(0)
    end_x(1, 0)
    end_x(1, 2)
    step(2)
    end_x(1, 1)
    finish(1)
    end_x(2, 0)
    end_x(2, 2)
    end_x(2, 1)
    finish(2)
    flush()


def tiles(a):
    return a.reshape(2, 8, TILES, 128).transpose(0, 2, 1, 3).reshape(CX * TILES, 128)


def body(pressure, previous, velocity, tucker_core, first_factor, second_factor, depth_factor):
    args = (tiles(pressure), tiles(previous), tiles(velocity), tucker_core, first_factor, second_factor, depth_factor.T)
    args = args + constants()
    dma = pltpu.SemaphoreType.DMA
    image = pl.pallas_call(
        kernel,
        out_shape=pltpu.VMEM((CX * TILES, 128), F32),
        in_specs=[pl.BlockSpec(memory_space=pl.ANY)] * len(args),
        out_specs=pl.BlockSpec(memory_space=pltpu.VMEM),
        scratch_shapes=[
            pltpu.VMEM(a.shape, a.dtype) for a in args
        ]
        + [
            pltpu.VMEM((STEPS, 4, 4, 8, 1152), BF16),
            pltpu.VMEM((STEPS, 4, 4, 8, 1664), BF16),
            pltpu.VMEM((STEPS, 24 * 10 * 8, 128), F32),
            pltpu.VMEM((24 * 10 * 8, 128), F32),
            pltpu.VMEM((CX * TILES, 128), F32),
            pltpu.VMEM((CX * TILES, 128), F32),
            pltpu.VMEM((CX * TILES, 128), F32),
            pltpu.VMEM((CX * TILES, 128), F32),
            pltpu.VMEM((STEPS, 2, 5, 3, 16, 128), BF16),
            pltpu.VMEM((STEPS, 2, 5, 3, 16, 128), BF16),
            pltpu.VMEM((STEPS, 2, 2, CX, 128), F32),
            pltpu.VMEM((STEPS, 2, 2, CX, 128), F32),
            pltpu.VMEM((128, 128), F32),
            pltpu.VMEM((24, 512), F32),
            pltpu.VMEM((96, 512), F32),
            pltpu.VMEM((STEPS, YL, 512), F32),
            pltpu.VMEM((2 * 8 * YL, 128), F32),
            pltpu.VMEM((256, 512), BF16),
            pltpu.VMEM((32, 128), BF16),
            pltpu.VMEM((64, 128), BF16),
            pltpu.VMEM((4, YL, 192), BF16),
            pltpu.VMEM((CX, 384), BF16),
            pltpu.VMEM((STEPS, CX, 768), F32),
            pltpu.VMEM((STEPS, CX, 768), F32),
            pltpu.VMEM((STEPS, CX, 768), F32),
            dma((len(args),)),
            dma((STEPS, 3)), dma((STEPS, 4)),
            dma((STEPS, 4)), dma((STEPS, 4)),
            dma((STEPS + 1,)), dma((STEPS + 1,)),
            dma((STEPS, 3)), dma((STEPS, 3)),
            dma((STEPS, 3, 4)), dma((STEPS, 3, 4)),
            dma((STEPS, 2)), dma((STEPS, 2)),
            dma((STEPS, 2)), dma((STEPS, 2)),
        ],
        compiler_params=pltpu.CompilerParams(
            collective_id=0, has_side_effects=True, vmem_limit_bytes=60 << 20
        ),
        name="image_steps",
    )(*args)
    return image.reshape(2, TILES, 8, 128).transpose(0, 2, 1, 3).reshape(CX, 8 * TILES * 16)


def solution(mesh):
    placed = (
        P("gx", "gy"),
        P("gx", "gy"),
        P("gx", "gy"),
        P(None, "gx", "gy"),
        P("gx", None),
        P("gy", None),
        P(),
    )
    return jax.shard_map(body, mesh=mesh, in_specs=placed, out_specs=P("gx", "gy"), check_vma=False)
```
